512 devices in a mesh: loop: 128 (over y, x, z_hi), narrow: 4 (over z_lo, core).
Axes of the slice: x: 4, y: 8, z: 8 (z_hi: 4, z_lo: 2; z = z_hi * 2 + z_lo), core: 2. Of those that a mesh axis runs over, the one named last changes fastest.
Arguments:
- picture_vectors: bfloat16 [114688, 1152], P(('loop', 'narrow')), may hold values from -0.1796875 to 0.1796875
- caption_vectors: bfloat16 [114688, 1152], P(('loop', 'narrow')), may hold values from -0.1796875 to 0.1796875
- caption_position: int32 [128, 896], P('loop'), may hold values from 0 to 895, each once within a row
- sharpness_factor: float32 [1], replicated, may hold values from 4 to 12
- affine_offset: float32 [1], replicated, may hold values from -3 to -1
Outputs:
- image_grad: float32 [114688, 1152], P(('loop', 'narrow'))
- text_grad: float32 [114688, 1152], P(('loop', 'narrow'))
The draws below stay inside these ranges and needn't reach their ends.
Inputs may be any that keep to these rules, and one draw needn't show every extreme that they name: Each row of caption_position is a permutation of 0 to 895.
All inputs are finite; a program needn't handle non-finite values.
Results may differ from the reference program's by a relative error of at most 0.014.
Values may be sent and summed in bfloat16 or wider, within the bound.
No kernel may reach another device: no remote copies, remote signals or barrier semaphores. Data moves between devices by JAX's collectives and lax.ppermute only.
A program may use at most 64 MiB of HBM per device.

```python
import math
import jax
import jax.numpy as jnp
from jax import lax

D = 1152
ROWS_DEV = 224
GROUP = 896
BATCH = 114688
N_LOOP = 128
N_NARROW = 4


def steps_of(key, dims, cuts, least, high):
    def one(axis_at, shards_of):
        steps = jax.random.uniform(jax.random.fold_in(jax.random.fold_in(key, 6), axis_at), (shards_of,), jnp.float32, least / len(cuts), high / len(cuts))
        return jnp.repeat(jnp.exp(steps), dims[axis_at] // shards_of).reshape((-1,) + (1,) * (len(dims) - axis_at - 1))

    loudness = one(*cuts[0])
    for cut in cuts[1:]:
        loudness = loudness * one(*cut)
    return loudness


def normal_values(own_key, shape, width, reach, pieces=(), dtype=jnp.bfloat16):
    factor_of = steps_of(own_key, shape, pieces, -0.22, 0.18) if pieces else 1.0
    entries = jax.random.normal(own_key, shape, jnp.float32) * width * factor_of
    return jnp.minimum(jnp.maximum(entries, -reach), reach).astype(dtype)


def setup_inputs(seed: int = 0) -> dict:
    arg_keys = jax.random.split(jax.random.key(seed), 6)
    picture_vectors = normal_values(arg_keys[0], (BATCH, D), 0.03, 0.1796875, ((0, 512),))
    caption_vectors = normal_values(arg_keys[1], (BATCH, D), 0.03, 0.1796875, ((0, 512),))
    caption_position = jax.vmap(lambda own: jax.random.permutation(own, GROUP))(jax.random.split(arg_keys[2], N_LOOP)).reshape((N_LOOP, GROUP)).astype(jnp.int32)
    sharpness_factor = jnp.clip(jnp.exp(jax.random.uniform(arg_keys[3], (1,), jnp.float32, math.log(4.0), math.log(12.0))), 4.0, 12.0)
    affine_offset = jnp.clip(jax.random.uniform(arg_keys[4], (1,), jnp.float32, -3.0, -1.0), -3.0, -1.0)
    return {"picture_vectors": picture_vectors, "caption_vectors": caption_vectors, "caption_position": caption_position, "sharpness_factor": sharpness_factor, "affine_offset": affine_offset}


def unit_rows(rows):
    values = rows.astype(jnp.float32)
    inv = lax.rsqrt(lax.optimization_barrier(jnp.sum(values * values, axis=-1, keepdims=True)) + 1e-06)
    return (values * inv, inv)

def reference(picture_vectors, caption_vectors, caption_position, sharpness_factor, affine_offset):
    score_multiplier = sharpness_factor[0]
    shift_b = affine_offset[0]
    img_unit, img_inv = unit_rows(picture_vectors)
    txt_unit, text_inverse_norm = unit_rows(caption_vectors)
    img_b = img_unit.astype(jnp.bfloat16).reshape(N_LOOP, GROUP, D)
    txt_b = txt_unit.astype(jnp.bfloat16).reshape(N_LOOP, GROUP, D)
    txt_prev = jnp.roll(txt_b, 1, axis=0)

    def single_group(items):
        img_g, txt_own, caption_arriving, pairs = items
        column_count = lax.broadcasted_iota(jnp.int32, (GROUP, GROUP), 1)
        positive = (column_count == pairs[:, None]).astype(jnp.float32)
        matched_logit = score_multiplier * jnp.dot(img_g, txt_own.T, preferred_element_type=jnp.float32) + shift_b
        visiting_logit = score_multiplier * jnp.dot(img_g, caption_arriving.T, preferred_element_type=jnp.float32) + shift_b
        matched_gradient = (score_multiplier * (jax.nn.sigmoid(matched_logit) - positive)).astype(jnp.bfloat16)
        vis_grad = (score_multiplier * jax.nn.sigmoid(visiting_logit)).astype(jnp.bfloat16)
        dimg = jnp.dot(matched_gradient, txt_own, preferred_element_type=jnp.float32)
        dimg = dimg + jnp.dot(vis_grad, caption_arriving, preferred_element_type=jnp.float32)
        img_f = img_g.astype(jnp.float32).reshape(N_NARROW, ROWS_DEV, D)
        own_f = matched_gradient.astype(jnp.float32).reshape(N_NARROW, ROWS_DEV, GROUP)
        vis_f = vis_grad.astype(jnp.float32).reshape(N_NARROW, ROWS_DEV, GROUP)
        own_terms = jnp.einsum('nrk,nrd->nkd', own_f, img_f).astype(jnp.bfloat16).astype(jnp.float32)
        vis_terms = jnp.einsum('nrk,nrd->nkd', vis_f, img_f).astype(jnp.bfloat16).astype(jnp.float32)
        return (dimg, lax.optimization_barrier(jnp.sum(own_terms, axis=0)), lax.optimization_barrier(jnp.sum(vis_terms, axis=0)))
    dimg, own_sum, vis_sum = lax.map(single_group, (img_b, txt_b, txt_prev, caption_position))
    txt_dunit = own_sum + jnp.roll(vis_sum, -1, axis=0)
    img_dunit = dimg.reshape(BATCH, D)
    txt_dunit = txt_dunit.reshape(BATCH, D)
    image_grad = (img_dunit - img_unit * lax.optimization_barrier(jnp.sum(img_unit * img_dunit, axis=-1, keepdims=True))) * img_inv
    text_grad = (txt_dunit - txt_unit * lax.optimization_barrier(jnp.sum(txt_unit * txt_dunit, axis=-1, keepdims=True))) * text_inverse_norm
    return (image_grad, text_grad)
```

```python
import functools

import jax
import jax.numpy as jnp
from jax import lax
from jax.experimental import pallas as pl
from jax.experimental.pallas import tpu as pltpu
from jax.sharding import PartitionSpec as P

AXES = ("loop", "narrow")
VMEM = pl.BlockSpec(memory_space=pltpu.VMEM)
SMEM = pl.BlockSpec(memory_space=pltpu.SMEM)
NT = (((1,), (1,)), ((), ()))
NN = (((1,), (0,)), ((), ()))


def inv_norm(values):
    return lax.rsqrt(jnp.sum(values * values, axis=-1, keepdims=True) + 1e-06)


def dot(a, b, dims):
    return lax.dot_general(a, b, dims, preferred_element_type=jnp.float32)


def call(body, out_shape, n_smem, n_vmem, flops=0):
    return pl.pallas_call(
        body,
        out_shape=out_shape,
        in_specs=[SMEM] * n_smem + [VMEM] * n_vmem,
        out_specs=jax.tree.map(lambda _: VMEM, out_shape),
        compiler_params=pltpu.CompilerParams(vmem_limit_bytes=32 * 1024 * 1024),
        cost_estimate=pl.CostEstimate(
            flops=flops, bytes_accessed=4 * 1024 * 1024, transcendentals=0
        ),
    )


def unit_body(odd, img, txt, p, q, pq):
    rows = img.shape[0]

    def unit(ref):
        values = ref[...].astype(jnp.float32)
        return (values * inv_norm(values)).astype(jnp.bfloat16)

    def put(first, second):
        p[...] = first
        q[...] = second
        pq[:rows] = first
        pq[rows:] = second

    img_b, txt_b = unit(img), unit(txt)

    @pl.when(odd[0] == 0)
    def _():
        put(img_b, txt_b)

    @pl.when(odd[0] == 1)
    def _():
        put(txt_b, img_b)


def weights(x, y, scale, shift):
    return scale * lax.logistic(scale * dot(x, y, NT) + shift)


def add_terms(x, ys, scale, shift):
    total = None
    for y in ys:
        term = dot(weights(x, y, scale, shift).astype(jnp.bfloat16), y, NN)
        total = term if total is None else total + term
    return total


def add_own(x, ys, u, v, scale, shift):
    total = None
    for j, y in enumerate(ys):
        positive = (u == v[j : j + 1]).astype(jnp.float32)
        g = scale * (lax.logistic(scale * dot(x, y, NT) + shift) - positive)
        term = dot(g.astype(jnp.bfloat16), y, NN)
        total = term if total is None else total + term
    return total


def early_body(scale, shift, p, x2, y0, y0c, part_p, part_x):
    ys = [y0[...], y0c[...]]
    part_x[...] = add_terms(x2[...], ys, scale[0], shift[0])
    part_p[...] = add_terms(p[...], ys, scale[0], shift[0])


def own_q_body(scale, shift, q, pq_c, p, x2, x2c, u, v, out):
    rows = q.shape[0]
    ys = [p[...], pq_c[:rows], x2[...], x2c[...]]
    out[...] = add_own(q[...], ys, u[...], v[...], scale[0], shift[0])


def late_body(scale, shift, x2, y1, y1c, part_x, out):
    ys = [y1[...], y1c[...]]
    out[...] = (part_x[...] + add_terms(x2[...], ys, scale[0], shift[0])).astype(jnp.bfloat16)


def tangent(raw, dunit):
    values = raw.astype(jnp.float32)
    inv = inv_norm(values)
    unit = values * inv
    return (dunit - unit * jnp.sum(unit * dunit, axis=-1, keepdims=True)) * inv


def rest_p_body(scale, shift, odd, img, txt, p, y1, y1c, part_p, q, pq_c, w2, w2c, u, v, out):
    rows = p.shape[0]
    x = p[...]
    total = part_p[...] + add_terms(x, [y1[...], y1c[...]], scale[0], shift[0])
    ys = [q[...], pq_c[rows:], w2[...], w2c[...]]
    total = total + add_own(x, ys, u[...], v[...], scale[0], shift[0])

    @pl.when(odd[0] == 0)
    def _():
        out[...] = tangent(img[...], total)

    @pl.when(odd[0] == 1)
    def _():
        out[...] = tangent(txt[...], total)


def last_body(odd, img, txt, own_q, back, grad_p, img_grad, txt_grad):
    total = own_q[...] + back[...].astype(jnp.float32)

    @pl.when(odd[0] == 0)
    def _():
        img_grad[...] = grad_p[...]
        txt_grad[...] = tangent(txt[...], total)

    @pl.when(odd[0] == 1)
    def _():
        img_grad[...] = tangent(img[...], total)
        txt_grad[...] = grad_p[...]


def local(picture_vectors, caption_vectors, caption_position, sharpness_factor, affine_offset):
    groups = lax.axis_size("loop")
    rows, depth = picture_vectors.shape
    img, txt, scale, shift = picture_vectors, caption_vectors, sharpness_factor, affine_offset

    def swap(to):
        pairs = []
        for g in range(groups):
            for n in range(4):
                h, m = to(g, n)
                pairs.append((g * 4 + n, (h % groups) * 4 + m))
        return lambda x: lax.ppermute(x, AXES, pairs)

    core = swap(lambda g, n: (g, n ^ 1))
    chip = swap(lambda g, n: (g, n ^ 2))
    group = swap(lambda g, n: (g + 1, n - 2) if n >= 2 else (g - 1, n + 2))

    here = lax.axis_index("narrow")
    odd = here // 2
    odd1 = odd.reshape(1).astype(jnp.int32)
    block = jax.ShapeDtypeStruct((rows, depth), jnp.bfloat16)
    wide = jax.ShapeDtypeStruct((rows, depth), jnp.float32)
    both = jax.ShapeDtypeStruct((2 * rows, depth), jnp.bfloat16)

    p, q, pq = call(unit_body, (block, block, both), 1, 2)(odd1, img, txt)
    x2 = chip(q)
    y0 = group(p)
    pq_c = core(pq)

    order = here ^ jnp.arange(4, dtype=jnp.int32)
    matches = caption_position.reshape(4, rows)[order]
    places = order[:, None] * rows + jnp.arange(rows, dtype=jnp.int32)[None, :]
    is_odd = odd == 1
    u_p = jnp.where(is_odd, places[0], matches[0])[:, None]
    u_q = jnp.where(is_odd, matches[0], places[0])[:, None]
    v_p = jnp.where(is_odd, matches, places)
    v_q = jnp.where(is_odd, places, matches)

    y1 = group(x2)
    w2 = chip(p)
    y0c = core(y0)
    x2c = core(x2)
    unit_flops = 4 * rows * rows * depth
    part_p, part_x = call(early_body, (wide, wide), 2, 4, 4 * unit_flops)(
        scale, shift, p, x2, y0, y0c
    )
    own_q = call(own_q_body, wide, 2, 7, 4 * unit_flops)(
        scale, shift, q, pq_c, p, x2, x2c, u_q, v_q
    )
    w2c = core(w2)
    y1c = core(y1)
    send = call(late_body, block, 2, 4, 2 * unit_flops)(scale, shift, x2, y1, y1c, part_x)
    back = chip(send)
    grad_p = call(rest_p_body, wide, 3, 12, 6 * unit_flops)(
        scale, shift, odd1, img, txt, p, y1, y1c, part_p, q, pq_c, w2, w2c, u_p, v_p
    )
    return call(last_body, (wide, wide), 1, 5)(odd1, img, txt, own_q, back, grad_p)


def solution(mesh):
    return jax.shard_map(
        local,
        mesh=mesh,
        in_specs=(
            P(AXES, None),
            P(AXES, None),
            P("loop", None),
            P(),
            P(),
        ),
        out_specs=(P(AXES, None), P(AXES, None)),
        check_vma=False,
    )
```

```python
import jax
import jax.numpy as jnp
from jax import lax
from jax.experimental import pallas as pl
from jax.experimental.pallas import tpu as pltpu
from jax.sharding import PartitionSpec as P

AXES = ("loop", "narrow")
VMEM = pl.BlockSpec(memory_space=pltpu.VMEM)
SMEM = pl.BlockSpec(memory_space=pltpu.SMEM)
HBM = pl.BlockSpec(memory_space=pltpu.HBM)
NT = (((1,), (1,)), ((), ()))
NN = (((1,), (0,)), ((), ()))
PIECES = 2
JOIN = 8 * 10**9


def inv_norm(values):
    return lax.rsqrt(jnp.sum(values * values, axis=-1, keepdims=True) + 1e-06)


def dot(a, b, dims):
    return lax.dot_general(a, b, dims, preferred_element_type=jnp.float32)


def call(body, out_shape, in_specs, out_specs=None, vmem=6, flops=1, **kwargs):
    if out_specs is None:
        out_specs = jax.tree.map(lambda _: VMEM, out_shape)
    return pl.pallas_call(
        body,
        out_shape=out_shape,
        in_specs=in_specs,
        out_specs=out_specs,
        compiler_params=pltpu.CompilerParams(vmem_limit_bytes=vmem * 1024 * 1024),
        cost_estimate=pl.CostEstimate(
            flops=flops, bytes_accessed=1, transcendentals=0
        ),
        **kwargs,
    )


def unit_body(odd, img, txt, p, q, raw, sems):
    rows = img.shape[0]
    size = rows // PIECES
    copies = []
    for j in range(PIECES):
        part = pl.ds(j * size, size)
        for i, ref in enumerate((img, txt)):
            copies.append(
                pltpu.make_async_copy(ref.at[part], raw.at[i, part], sems.at[2 * j + i])
            )
    for copy in copies:
        copy.start()
    for j in range(PIECES):
        part = pl.ds(j * size, size)
        unit = []
        for i in range(2):
            copies[2 * j + i].wait()
            values = raw[i, part].astype(jnp.float32)
            unit.append((values * inv_norm(values)).astype(jnp.bfloat16))

        @pl.when(odd[0] == 0)
        def _():
            p[part] = unit[0]
            q[part] = unit[1]

        @pl.when(odd[0] == 1)
        def _():
            p[part] = unit[1]
            q[part] = unit[0]


def terms(x, ys, scale, shift, positive=None):
    total = None
    for j, y in enumerate(ys):
        g = lax.logistic(scale * dot(x, y, NT) + shift)
        if positive is not None:
            u, v = positive
            g = g - (u == v[j]).astype(jnp.float32)
        term = dot((scale * g).astype(jnp.bfloat16), y, NN)
        total = term if total is None else total + term
    return total


def first_body(scale, shift, p, q, u_p, v_p, u_q, v_q, sum_p, sum_q, again, pq):
    rows = p.shape[0]
    x, y = p[...], q[...]
    again[...] = x
    pq[:rows] = x
    pq[rows:] = y
    sum_p[...] = terms(x, [y], scale[0], shift[0], (u_p[...], [v_p[:1]]))
    sum_q[...] = terms(y, [x], scale[0], shift[0], (u_q[...], [v_q[:1]]))


def join_body(x2, y0, xy):
    rows = x2.shape[0]
    xy[:rows] = x2[...]
    xy[rows:] = y0[...]


def near_body(scale, shift, p, q, pq_c, xy, u_p, v_p, u_q, v_q, own_p, own_q, sum_p, sum_q):
    rows = p.shape[0]
    x_c, y_c, x2 = pq_c[:rows], pq_c[rows:], xy[:rows]
    sum_p[...] = own_p[...] + terms(p[...], [y_c], scale[0], shift[0], (u_p[...], [v_p[1:2]]))
    own = (u_q[...], [v_q[1:2], v_q[2:3]])
    sum_q[...] = own_q[...] + terms(q[...], [x_c, x2], scale[0], shift[0], own)


def pair_body(y1, w2, _sum, yw):
    rows = y1.shape[0]
    yw[:rows] = y1[...]
    yw[rows:] = w2[...]


def mid_body(scale, shift, xy, xy_c, y1, part):
    rows = y1.shape[0]
    ys = [xy[rows:], xy_c[rows:], y1[...]]
    part[...] = terms(xy[:rows], ys, scale[0], shift[0])


def late_body(scale, shift, x2, yw_c, part, out):
    rows = x2.shape[0]
    out[...] = (part[...] + terms(x2[...], [yw_c[:rows]], scale[0], shift[0])).astype(out.dtype)


def tangent(raw, dunit):
    values = raw.astype(jnp.float32)
    inv = inv_norm(values)
    unit = values * inv
    return (dunit - unit * jnp.sum(unit * dunit, axis=-1, keepdims=True)) * inv


def write_out(is_txt, img, txt, dunit, img_grad, txt_grad, held, sems):
    rows = img.shape[0]
    size = rows // PIECES

    def go(raw, grad):
        copies = []
        for j in range(PIECES):
            part = pl.ds(j * size, size)
            held[part] = tangent(raw[part], dunit(part))
            copies.append(pltpu.make_async_copy(held.at[part], grad.at[part], sems.at[j]))
            copies[-1].start()
        for copy in copies:
            copy.wait()

    @pl.when(jnp.logical_not(is_txt))
    def _():
        go(img, img_grad)

    @pl.when(is_txt)
    def _():
        go(txt, txt_grad)


def rest_body(
    scale, shift, odd, img, txt, p, q, xy, xy_c, yw, yw_c, u_p, v_p, u_q, v_q, own_p, own_q,
    sum_q, img_grad, txt_grad, total, held, sems
):
    rows = p.shape[0]
    x = p[...]
    own = (u_q[...], [v_q[3:]])
    sum_q[...] = own_q[...] + terms(q[...], [xy_c[:rows]], scale[0], shift[0], own)
    own = (u_p[...], [v_p[2:3], v_p[3:]])
    visiting = [xy[rows:], xy_c[rows:], yw[:rows], yw_c[:rows]]
    total[...] = (
        own_p[...]
        + terms(x, visiting, scale[0], shift[0])
        + terms(x, [yw[rows:], yw_c[rows:]], scale[0], shift[0], own)
    )
    write_out(odd[0] == 1, img, txt, lambda part: total[part], img_grad, txt_grad, held, sems)


def last_body(odd, img, txt, sum_q, back, _img, _txt, img_grad, txt_grad, held, sems):
    def dunit(part):
        return sum_q[part] + back[part].astype(jnp.float32)

    write_out(odd[0] == 0, img, txt, dunit, img_grad, txt_grad, held, sems)


def local(picture_vectors, caption_vectors, caption_position, sharpness_factor, affine_offset):
    groups = lax.axis_size("loop")
    rows, depth = picture_vectors.shape
    img, txt, scale, shift = picture_vectors, caption_vectors, sharpness_factor, affine_offset

    def swap(to):
        pairs = []
        for g in range(groups):
            for n in range(4):
                h, m = to(g, n)
                pairs.append((g * 4 + n, (h % groups) * 4 + m))
        return lambda x: lax.ppermute(x, AXES, pairs)

    core = swap(lambda g, n: (g, n ^ 1))
    chip = swap(lambda g, n: (g, n ^ 2))
    group = swap(lambda g, n: (g + 1, n - 2) if n >= 2 else (g - 1, n + 2))

    here = lax.axis_index("narrow")
    odd = here // 2
    odd1 = odd.reshape(1).astype(jnp.int32)
    block = jax.ShapeDtypeStruct((rows, depth), jnp.bfloat16)
    wide = jax.ShapeDtypeStruct((rows, depth), jnp.float32)
    both = jax.ShapeDtypeStruct((2 * rows, depth), jnp.bfloat16)

    dma = pltpu.SemaphoreType.DMA
    far = lambda x: pltpu.with_memory_space_constraint(x, pltpu.HBM)
    p, q = call(
        unit_body,
        (block, block),
        [SMEM, HBM, HBM],
        scratch_shapes=[pltpu.VMEM((2, rows, depth), jnp.bfloat16), dma((2 * PIECES,))],
    )(odd1, far(img), far(txt))
    x2 = chip(q)
    y0 = group(p)

    order = here ^ jnp.arange(4, dtype=jnp.int32)
    matches = caption_position.reshape(4, rows)[order]
    places = order[:, None] * rows + jnp.arange(rows, dtype=jnp.int32)[None, :]
    is_odd = odd == 1
    u_p = jnp.where(is_odd, places[0], matches[0])[:, None]
    u_q = jnp.where(is_odd, matches[0], places[0])[:, None]
    v_p = jnp.where(is_odd, matches, places)
    v_q = jnp.where(is_odd, places, matches)

    sums = (wide, wide)
    match = (u_p, v_p, u_q, v_q)
    sum_p, sum_q, again, pq = call(first_body, sums + (block, both), [SMEM] * 2 + [VMEM] * 6)(
        scale, shift, p, q, *match
    )
    pq_c = core(pq)
    w2 = chip(again)
    y1 = group(x2)
    xy = call(join_body, both, [VMEM] * 2, flops=JOIN)(x2, y0)
    xy_c = core(xy)
    sum_p, sum_q = call(near_body, sums, [SMEM] * 2 + [VMEM] * 10)(
        scale, shift, p, q, pq_c, xy, *match, sum_p, sum_q
    )
    yw = call(pair_body, both, [VMEM] * 3)(y1, w2, sum_q)
    yw_c = core(yw)
    part = call(mid_body, wide, [SMEM] * 2 + [VMEM] * 3)(scale, shift, xy, xy_c, y1)
    send = call(late_body, block, [SMEM] * 2 + [VMEM] * 3)(scale, shift, x2, yw_c, part)
    back = chip(send)
    out = [pltpu.VMEM((rows, depth), jnp.float32), dma((PIECES,))]
    sum_q, *grads = call(
        rest_body,
        (wide,) * 3,
        [SMEM] * 3 + [VMEM] * 14,
        (VMEM, HBM, HBM),
        scratch_shapes=[pltpu.VMEM((rows, depth), jnp.float32)] + out,
    )(scale, shift, odd1, img, txt, p, q, xy, xy_c, yw, yw_c, *match, sum_p, sum_q)
    return call(
        last_body,
        (wide, wide),
        [SMEM] + [VMEM] * 4 + [HBM] * 2,
        (HBM, HBM),
        scratch_shapes=out,
        input_output_aliases={5: 0, 6: 1},
    )(odd1, img, txt, sum_q, back, *grads)


def solution(mesh):
    return jax.shard_map(
        local,
        mesh=mesh,
        in_specs=(
            P(AXES, None),
            P(AXES, None),
            P("loop", None),
            P(),
            P(),
        ),
        out_specs=(P(AXES, None), P(AXES, None)),
        check_vma=False,
    )
```

```python
import jax
import jax.numpy as jnp
from jax import lax
from jax.experimental import pallas as pl
from jax.experimental.pallas import tpu as pltpu
from jax.sharding import PartitionSpec as P

AXES = ("loop", "narrow")
VMEM = pl.BlockSpec(memory_space=pltpu.VMEM)
SMEM = pl.BlockSpec(memory_space=pltpu.SMEM)
HBM = pl.BlockSpec(memory_space=pltpu.HBM)
NT = (((1,), (1,)), ((), ()))
NN = (((1,), (0,)), ((), ()))
PIECES = 2
COST = {"pair": 32 * 10**9, "mid": 8 * 10**9, "late": 64 * 10**9, "visit": 32 * 10**9, "last": 4 * 10**9}


def inv_norm(values):
    return lax.rsqrt(jnp.sum(values * values, axis=-1, keepdims=True) + 1e-06)


def dot(a, b, dims):
    return lax.dot_general(a, b, dims, preferred_element_type=jnp.float32)


def call(body, out_shape, in_specs, out_specs=None, vmem=6, **kwargs):
    if out_specs is None:
        out_specs = jax.tree.map(lambda _: VMEM, out_shape)
    name = body.__name__.removesuffix("_body")
    return pl.pallas_call(
        body,
        name=name,
        out_shape=out_shape,
        in_specs=in_specs,
        out_specs=out_specs,
        compiler_params=pltpu.CompilerParams(vmem_limit_bytes=vmem * 1024 * 1024),
        cost_estimate=pl.CostEstimate(flops=COST.get(name, 1), bytes_accessed=1, transcendentals=0),
        **kwargs,
    )


def unit_body(odd, img, txt, p, q_lo, q_hi, raw, sems):
    rows = img.shape[0]
    size = rows // PIECES
    half = rows // 2
    copies = []
    for j in range(PIECES):
        part = pl.ds(j * size, size)
        for i, ref in enumerate((img, txt)):
            copies.append(
                pltpu.make_async_copy(ref.at[part], raw.at[i, part], sems.at[2 * j + i])
            )
    for copy in copies:
        copy.start()
    for j in range(PIECES):
        part = pl.ds(j * size, size)
        unit = []
        for i in range(2):
            copies[2 * j + i].wait()
            values = raw[i, part].astype(jnp.float32)
            unit.append((values * inv_norm(values)).astype(jnp.bfloat16))
        q, start = (q_lo, j * size) if j * size < half else (q_hi, j * size - half)

        def put(first, second):
            p[part] = first
            q[pl.ds(start, size)] = second

        @pl.when(odd[0] == 0)
        def _():
            put(unit[0], unit[1])

        @pl.when(odd[0] == 1)
        def _():
            put(unit[1], unit[0])


def match_body(here, scale, shift, pos, sc, u_p, v_p, u_q, v_q):
    rows = u_p.shape[0]
    sc[0:1] = jnp.full((1, sc.shape[1]), scale[0], jnp.float32)
    sc[1:2] = jnp.full((1, sc.shape[1]), shift[0], jnp.float32)
    me = here[0]
    lane = lax.broadcasted_iota(jnp.int32, (1, rows), 1)
    square = (rows, rows)
    diagonal = lax.broadcasted_iota(jnp.int32, square, 0) == lax.broadcasted_iota(
        jnp.int32, square, 1
    )

    def column(row):
        spread = jnp.where(diagonal, jnp.broadcast_to(row, square).astype(jnp.float32), 0.0)
        return jnp.sum(spread, axis=1, keepdims=True).astype(jnp.int32)

    matches, places = [], []
    for j in range(4):
        block = me ^ j
        matches.append(pos[pl.ds(block, 1)])
        places.append(block * rows + lane)

    def put(u_img, v_img, u_txt, v_txt):
        u_img[...] = column(matches[0])
        u_txt[...] = column(places[0])
        for j in range(4):
            v_img[j : j + 1] = places[j]
            v_txt[j : j + 1] = matches[j]

    @pl.when(me < 2)
    def _():
        put(u_p, v_p, u_q, v_q)

    @pl.when(me >= 2)
    def _():
        put(u_q, v_q, u_p, v_p)


def terms(x, ys, sc, positive=None):
    scale, shift = sc[0:1, 0:1], sc[1:2, 0:1]
    total = None
    for j, y in enumerate(ys):
        g = lax.logistic(scale * dot(x, y, NT) + shift)
        if positive is not None:
            u, v = positive
            g = g - (u == v[j]).astype(jnp.float32)
        term = dot((scale * g).astype(jnp.bfloat16), y, NN)
        total = term if total is None else total + term
    return total


def join_body(p, q_lo, q_hi, x2_lo, x2_hi, y0, out):
    row = 0
    for part in (p, q_lo, q_hi, x2_lo, x2_hi, y0):
        out[pl.ds(row, part.shape[0])] = part[...]
        row += part.shape[0]


def pair_body(y_lo, y_hi, _w2, y1):
    half = y_lo.shape[0]
    y1[:half] = y_lo[...]
    y1[half:] = y_hi[...]


def block(ref, j):
    rows = ref.shape[0] // 4
    return ref[j * rows : (j + 1) * rows]


def mid_body(sc, near, near_c, y1, part):
    part[...] = terms(block(near, 2), [block(near, 3), block(near_c, 3), y1[...]], sc)


def late_body(sc, near, y1_c, part, out):
    out[...] = (part[...] + terms(block(near, 2), [y1_c[...]], sc)).astype(out.dtype)


def tangent(raw, dunit):
    values = raw.astype(jnp.float32)
    inv = inv_norm(values)
    unit = values * inv
    return (dunit - unit * jnp.sum(unit * dunit, axis=-1, keepdims=True)) * inv


def write_out(is_txt, img, txt, dunit, img_grad, txt_grad, held, sems):
    rows = img.shape[0]
    size = rows // PIECES

    def go(raw, grad):
        copies = []
        for j in range(PIECES):
            part = pl.ds(j * size, size)
            held[part] = tangent(raw[part], dunit(part))
            copies.append(pltpu.make_async_copy(held.at[part], grad.at[part], sems.at[j]))
            copies[-1].start()
        for copy in copies:
            copy.wait()

    @pl.when(jnp.logical_not(is_txt))
    def _():
        go(img, img_grad)

    @pl.when(is_txt)
    def _():
        go(txt, txt_grad)


def visit_body(
    sc, near, near_c, y1, y1_c, w2, _send, u_p, v_p, u_q, v_q, sum_p, sum_q, w2_lo, w2_hi
):
    half = w2_lo.shape[0]
    w2_lo[...] = w2[:half]
    w2_hi[...] = w2[half:]
    x, y, x2, y0 = (block(near, j) for j in range(4))
    x_c, y_c, x2_c, y0_c = (block(near_c, j) for j in range(4))
    columns = [v_p[j : j + 1] for j in range(3)]
    sum_p[...] = terms(x, [y, y_c, w2[...]], sc, (u_p[...], columns)) + terms(
        x, [y0, y0_c, y1[...], y1_c[...]], sc
    )
    columns = [v_q[j : j + 1] for j in range(4)]
    sum_q[...] = terms(y, [x, x_c, x2, x2_c], sc, (u_q[...], columns))


def rest_body(
    sc, odd, img, txt, p, w2_lo_c, w2_hi_c, u_p, v_p, sum_p, img_grad, txt_grad, total, held, sems
):
    half = p.shape[0] // 2
    own = (u_p[...], [v_p[3:4, :half], v_p[3:4, half:]])
    total[...] = sum_p[...] + terms(p[...], [w2_lo_c[...], w2_hi_c[...]], sc, own)
    write_out(odd[0] == 1, img, txt, lambda part: total[part], img_grad, txt_grad, held, sems)


def last_body(odd, img, txt, sum_q, back, _img, _txt, img_grad, txt_grad, held, sems):
    def dunit(part):
        return sum_q[part] + back[part].astype(jnp.float32)

    write_out(odd[0] == 0, img, txt, dunit, img_grad, txt_grad, held, sems)


def local(picture_vectors, caption_vectors, caption_position, sharpness_factor, affine_offset):
    groups = lax.axis_size("loop")
    rows, depth = picture_vectors.shape
    half = rows // 2
    img, txt, scale, shift = picture_vectors, caption_vectors, sharpness_factor, affine_offset

    def swap(to):
        pairs = []
        for g in range(groups):
            for n in range(4):
                h, m = to(g, n)
                pairs.append((g * 4 + n, (h % groups) * 4 + m))
        def go(x, name):
            with jax.named_scope(name):
                return lax.ppermute(x, AXES, pairs)

        return go

    core = swap(lambda g, n: (g, n ^ 1))
    chip = swap(lambda g, n: (g, n ^ 2))
    group = swap(lambda g, n: (g + 1, n - 2) if n >= 2 else (g - 1, n + 2))

    def of(shape, dtype=jnp.float32):
        return jax.ShapeDtypeStruct(shape, dtype)

    here = lax.axis_index("narrow").astype(jnp.int32).reshape(1)
    odd = here // 2
    bf16 = jnp.bfloat16
    one, wide = of((rows, depth), bf16), of((rows, depth))
    part, four = of((half, depth), bf16), of((4 * rows, depth), bf16)
    dma = pltpu.SemaphoreType.DMA
    far = lambda x: pltpu.with_memory_space_constraint(x, pltpu.HBM)

    p, q_lo, q_hi = call(
        unit_body,
        (one, part, part),
        [SMEM, HBM, HBM],
        scratch_shapes=[pltpu.VMEM((2, rows, depth), bf16), dma((2 * PIECES,))],
    )(odd, far(img), far(txt))
    y0 = group(p, "group_p")
    x2_lo, x2_hi = chip(q_lo, "chip_lo"), chip(q_hi, "chip_hi")
    w2 = chip(p, "chip_p")
    y_lo, y_hi = group(x2_lo, "group_lo"), group(x2_hi, "group_hi")

    place = (of((rows, 1), jnp.int32), of((4, rows), jnp.int32))
    sc, *match = call(match_body, (of((2, 128)),) + place + place, [SMEM] * 3 + [VMEM])(
        here, scale, shift, caption_position.reshape(4, rows)
    )
    near = call(join_body, four, [VMEM] * 6)(p, q_lo, q_hi, x2_lo, x2_hi, y0)
    near_c = core(near, "core_xy")
    y1 = call(pair_body, one, [VMEM] * 3)(y_lo, y_hi, w2)
    y1_c = core(y1, "core_y")
    part_x = call(mid_body, wide, [VMEM] * 4)(sc, near, near_c, y1)
    send = call(late_body, one, [VMEM] * 4)(sc, near, y1_c, part_x)
    back = chip(send, "chip_send")
    sum_p, sum_q, w2_lo, w2_hi = call(visit_body, (wide, wide, part, part), [VMEM] * 11)(
        sc, near, near_c, y1, y1_c, w2, send, *match
    )
    out = [pltpu.VMEM((rows, depth), jnp.float32), dma((PIECES,))]
    grads = call(
        rest_body,
        (wide, wide),
        [VMEM, SMEM] + [VMEM] * 8,
        (HBM, HBM),
        scratch_shapes=[pltpu.VMEM((rows, depth), jnp.float32)] + out,
    )(sc, odd, img, txt, p, core(w2_lo, "core_w_lo"), core(w2_hi, "core_w_hi"), *match[:2], sum_p)
    return call(
        last_body,
        (wide, wide),
        [SMEM] + [VMEM] * 4 + [HBM] * 2,
        (HBM, HBM),
        scratch_shapes=out,
        input_output_aliases={5: 0, 6: 1},
    )(odd, img, txt, sum_q, back, *grads)


def solution(mesh):
    return jax.shard_map(
        local,
        mesh=mesh,
        in_specs=(
            P(AXES, None),
            P(AXES, None),
            P("loop", None),
            P(),
            P(),
        ),
        out_specs=(P(AXES, None), P(AXES, None)),
        check_vma=False,
    )
```

```python
import jax
import jax.numpy as jnp
from jax import lax
from jax.experimental import pallas as pl
from jax.experimental.pallas import tpu as pltpu
from jax.sharding import PartitionSpec as P

AXES = ("loop", "narrow")
VMEM = pl.BlockSpec(memory_space=pltpu.VMEM)
SMEM = pl.BlockSpec(memory_space=pltpu.SMEM)
HBM = pl.BlockSpec(memory_space=pltpu.HBM)
NT = (((1,), (1,)), ((), ()))
NN = (((1,), (0,)), ((), ()))
COST = {"pair": 16 * 10**9, "late": 8 * 10**9, "rest": 1 * 10**9, "last": 16 * 10**9}


def pieces_of(rows):
    half = rows // 2
    first = half // 32 * 16
    edges = [0, first, half, half + first, rows]
    return [(low, high - low) for low, high in zip(edges, edges[1:])]


def inv_norm(values):
    return lax.rsqrt(jnp.sum(values * values, axis=-1, keepdims=True) + 1e-06)


def dot(a, b, dims):
    return lax.dot_general(a, b, dims, preferred_element_type=jnp.float32)


def call(body, out_shape, in_specs, out_specs=None, vmem=6, **kwargs):
    if out_specs is None:
        out_specs = jax.tree.map(lambda _: VMEM, out_shape)
    name = body.__name__.removesuffix("_body")
    return pl.pallas_call(
        body,
        name=name,
        out_shape=out_shape,
        in_specs=in_specs,
        out_specs=out_specs,
        compiler_params=pltpu.CompilerParams(vmem_limit_bytes=vmem * 1024 * 1024),
        cost_estimate=pl.CostEstimate(flops=COST.get(name, 1), bytes_accessed=1, transcendentals=0),
        **kwargs,
    )


def unit_rows(take_txt, img, txt, outs, raw, sems):
    pieces = pieces_of(img.shape[0])

    def go(ref):
        copies = []
        for j, (start, size) in enumerate(pieces):
            part = pl.ds(start, size)
            copies.append(pltpu.make_async_copy(ref.at[part], raw.at[part], sems.at[j]))
            copies[-1].start()
        for copy, (start, size) in zip(copies, pieces):
            copy.wait()
            values = raw[pl.ds(start, size)].astype(jnp.float32)
            out = outs[start // outs[0].shape[0]]
            into = pl.ds(start % out.shape[0], size)
            out[into] = (values * inv_norm(values)).astype(jnp.bfloat16)

    @pl.when(jnp.logical_not(take_txt))
    def _():
        go(img)

    @pl.when(take_txt)
    def _():
        go(txt)


def unit_p_body(odd, img, txt, p, raw, sems):
    unit_rows(odd[0] == 1, img, txt, [p], raw, sems)


def unit_q_body(odd, img, txt, q_lo, q_hi, raw, sems):
    unit_rows(odd[0] == 0, img, txt, [q_lo, q_hi], raw, sems)


def match_body(here, scale, shift, pos, sc, u_p, v_p, u_q, v_q):
    rows = u_p.shape[0]
    sc[0:1] = jnp.full((1, sc.shape[1]), scale[0], jnp.float32)
    sc[1:2] = jnp.full((1, sc.shape[1]), shift[0], jnp.float32)
    me = here[0]
    lane = lax.broadcasted_iota(jnp.int32, (1, rows), 1)
    square = (rows, rows)
    diagonal = lax.broadcasted_iota(jnp.int32, square, 0) == lax.broadcasted_iota(
        jnp.int32, square, 1
    )

    def column(row):
        spread = jnp.where(diagonal, jnp.broadcast_to(row, square).astype(jnp.float32), 0.0)
        return jnp.sum(spread, axis=1, keepdims=True).astype(jnp.int32)

    matches, places = [], []
    for j in range(4):
        block = me ^ j
        matches.append(pos[pl.ds(block, 1)])
        places.append(block * rows + lane)

    def put(u_img, v_img, u_txt, v_txt):
        u_img[...] = column(matches[0])
        u_txt[...] = column(places[0])
        for j in range(4):
            v_img[j : j + 1] = places[j]
            v_txt[j : j + 1] = matches[j]

    @pl.when(me < 2)
    def _():
        put(u_p, v_p, u_q, v_q)

    @pl.when(me >= 2)
    def _():
        put(u_q, v_q, u_p, v_p)


def terms(x, ys, sc, positive=None):
    scale, shift = sc[0:1, 0:1], sc[1:2, 0:1]
    total = None
    for j, y in enumerate(ys):
        g = lax.logistic(scale * dot(x, y, NT) + shift)
        if positive is not None:
            u, v = positive
            g = g - (u == v[j]).astype(jnp.float32)
        term = dot((scale * g).astype(jnp.bfloat16), y, NN)
        total = term if total is None else total + term
    return total


def join_body(p, q_lo, q_hi, x2_lo, x2_hi, y0, out):
    row = 0
    for part in (p, q_lo, q_hi, x2_lo, x2_hi, y0):
        out[pl.ds(row, part.shape[0])] = part[...]
        row += part.shape[0]


def own_body(sc, near, u_p, v_p, u_q, v_q, sum_p, sum_q):
    x, y, x2, y0 = (block(near, j) for j in range(4))
    sum_p[...] = terms(x, [y], sc, (u_p[...], [v_p[0:1]])) + terms(x, [y0], sc)
    sum_q[...] = terms(y, [x, x2], sc, (u_q[...], [v_q[0:1], v_q[2:3]]))


def pair_body(y_lo, y_hi, _w2, _sum, y1):
    half = y_lo.shape[0]
    y1[:half] = y_lo[...]
    y1[half:] = y_hi[...]


def block(ref, j):
    rows = ref.shape[0] // 4
    return ref[j * rows : (j + 1) * rows]


def mid_body(sc, near, near_c, y1, part):
    part[...] = terms(block(near, 2), [block(near, 3), block(near_c, 3), y1[...]], sc)


def late_body(sc, near, y1_c, part, w2, out, w2_lo, w2_hi):
    half = w2_lo.shape[0]
    w2_lo[...] = w2[:half]
    w2_hi[...] = w2[half:]
    out[...] = (part[...] + terms(block(near, 2), [y1_c[...]], sc)).astype(out.dtype)


def tangent(raw, dunit):
    values = raw.astype(jnp.float32)
    inv = inv_norm(values)
    unit = values * inv
    return (dunit - unit * jnp.sum(unit * dunit, axis=-1, keepdims=True)) * inv


def write_out(is_txt, img, txt, dunit, img_grad, txt_grad, held, sems):
    def go(raw, grad):
        copies = []
        for j, (start, size) in enumerate(pieces_of(raw.shape[0])):
            part = pl.ds(start, size)
            held[part] = tangent(raw[part], dunit(part))
            copies.append(pltpu.make_async_copy(held.at[part], grad.at[part], sems.at[j]))
            copies[-1].start()
        for copy in copies:
            copy.wait()

    @pl.when(jnp.logical_not(is_txt))
    def _():
        go(img, img_grad)

    @pl.when(is_txt)
    def _():
        go(txt, txt_grad)


def visit_body(
    sc, near, near_c, y1, y1_c, w2, _send, u_p, v_p, u_q, v_q, own_p, own_q, sum_p, sum_q
):
    x, y = block(near, 0), block(near, 1)
    x_c, y_c, x2_c, y0_c = (block(near_c, j) for j in range(4))
    sum_p[...] = (
        own_p[...]
        + terms(x, [y_c, w2[...]], sc, (u_p[...], [v_p[1:2], v_p[2:3]]))
        + terms(x, [y0_c, y1[...], y1_c[...]], sc)
    )
    own = (u_q[...], [v_q[1:2], v_q[3:4]])
    sum_q[...] = own_q[...] + terms(y, [x_c, x2_c], sc, own)


def rest_body(
    sc, odd, img, txt, p, w2_lo_c, w2_hi_c, u_p, v_p, sum_p, img_grad, txt_grad, total, held, sems
):
    half = p.shape[0] // 2
    own = (u_p[...], [v_p[3:4, :half], v_p[3:4, half:]])
    total[...] = sum_p[...] + terms(p[...], [w2_lo_c[...], w2_hi_c[...]], sc, own)
    write_out(odd[0] == 1, img, txt, lambda part: total[part], img_grad, txt_grad, held, sems)


def last_body(odd, img, txt, sum_q, back, _img, _txt, img_grad, txt_grad, held, sems):
    def dunit(part):
        return sum_q[part] + back[part].astype(jnp.float32)

    write_out(odd[0] == 0, img, txt, dunit, img_grad, txt_grad, held, sems)


def local(picture_vectors, caption_vectors, caption_position, sharpness_factor, affine_offset):
    groups = lax.axis_size("loop")
    rows, depth = picture_vectors.shape
    half = rows // 2
    img, txt, scale, shift = picture_vectors, caption_vectors, sharpness_factor, affine_offset

    def swap(to):
        pairs = []
        for g in range(groups):
            for n in range(4):
                h, m = to(g, n)
                pairs.append((g * 4 + n, (h % groups) * 4 + m))
        def go(x, name):
            with jax.named_scope(name):
                return lax.ppermute(x, AXES, pairs)

        return go

    core = swap(lambda g, n: (g, n ^ 1))
    chip = swap(lambda g, n: (g, n ^ 2))
    group = swap(lambda g, n: (g + 1, n - 2) if n >= 2 else (g - 1, n + 2))

    def of(shape, dtype=jnp.float32):
        return jax.ShapeDtypeStruct(shape, dtype)

    here = lax.axis_index("narrow").astype(jnp.int32).reshape(1)
    odd = here // 2
    bf16 = jnp.bfloat16
    one, wide = of((rows, depth), bf16), of((rows, depth))
    part, four = of((half, depth), bf16), of((4 * rows, depth), bf16)
    dma = pltpu.SemaphoreType.DMA
    far = lambda x: pltpu.with_memory_space_constraint(x, pltpu.HBM)

    img_far, txt_far = far(img), far(txt)
    scratch = [pltpu.VMEM((rows, depth), bf16), dma((4,))]
    p = call(unit_p_body, one, [SMEM, HBM, HBM], scratch_shapes=scratch)(odd, img_far, txt_far)
    q_lo, q_hi = call(unit_q_body, (part, part), [SMEM, HBM, HBM], scratch_shapes=scratch)(
        odd, img_far, txt_far
    )
    y0 = group(p, "group_p")
    x2_lo, x2_hi = chip(q_lo, "chip_lo"), chip(q_hi, "chip_hi")
    w2 = chip(p, "chip_p")
    y_lo, y_hi = group(x2_lo, "group_lo"), group(x2_hi, "group_hi")

    place = (of((rows, 1), jnp.int32), of((4, rows), jnp.int32))
    sc, *match = call(match_body, (of((2, 128)),) + place + place, [SMEM] * 3 + [VMEM])(
        here, scale, shift, caption_position.reshape(4, rows)
    )
    near = call(join_body, four, [VMEM] * 6)(p, q_lo, q_hi, x2_lo, x2_hi, y0)
    near_c = core(near, "core_xy")
    own_p, own_q = call(own_body, (wide, wide), [VMEM] * 6)(sc, near, *match)
    y1 = call(pair_body, one, [VMEM] * 4)(y_lo, y_hi, w2, own_q)
    y1_c = core(y1, "core_y")
    part_x = call(mid_body, wide, [VMEM] * 4)(sc, near, near_c, y1)
    send, w2_lo, w2_hi = call(late_body, (one, part, part), [VMEM] * 5)(
        sc, near, y1_c, part_x, w2
    )
    back = chip(send, "chip_send")
    sum_p, sum_q = call(visit_body, (wide, wide), [VMEM] * 13)(
        sc, near, near_c, y1, y1_c, w2, send, *match, own_p, own_q
    )
    out = [pltpu.VMEM((rows, depth), jnp.float32), dma((4,))]
    grads = call(
        rest_body,
        (wide, wide),
        [VMEM, SMEM] + [VMEM] * 8,
        (HBM, HBM),
        scratch_shapes=[pltpu.VMEM((rows, depth), jnp.float32)] + out,
    )(sc, odd, img, txt, p, core(w2_lo, "core_w_lo"), core(w2_hi, "core_w_hi"), *match[:2], sum_p)
    return call(
        last_body,
        (wide, wide),
        [SMEM] + [VMEM] * 4 + [HBM] * 2,
        (HBM, HBM),
        scratch_shapes=out,
        input_output_aliases={5: 0, 6: 1},
    )(odd, img, txt, sum_q, back, *grads)


def solution(mesh):
    return jax.shard_map(
        local,
        mesh=mesh,
        in_specs=(
            P(AXES, None),
            P(AXES, None),
            P("loop", None),
            P(),
            P(),
        ),
        out_specs=(P(AXES, None), P(AXES, None)),
        check_vma=False,
    )
```

```python
import jax
import jax.numpy as jnp
from jax import lax
from jax.experimental import pallas as pl
from jax.experimental.pallas import tpu as pltpu
from jax.sharding import PartitionSpec as P

AXES = ("loop", "narrow")
VMEM = pl.BlockSpec(memory_space=pltpu.VMEM)
SMEM = pl.BlockSpec(memory_space=pltpu.SMEM)
HBM = pl.BlockSpec(memory_space=pltpu.HBM)
NT = (((1,), (1,)), ((), ()))
NN = (((1,), (0,)), ((), ()))
COST = {"unit": 16 * 10**9, "take": 64 * 10**9, "last": 64 * 10**9}


def pieces_of(rows):
    half = rows // 2
    first = half // 32 * 16
    edges = [0, first, half, half + first, rows]
    return [(low, high - low) for low, high in zip(edges, edges[1:])]


def inv_norm(values):
    return lax.rsqrt(jnp.sum(values * values, axis=-1, keepdims=True) + 1e-06)


def dot(a, b, dims):
    return lax.dot_general(a, b, dims, preferred_element_type=jnp.float32)


def call(body, out_shape, in_specs, out_specs=None, vmem=6, **kwargs):
    if out_specs is None:
        out_specs = jax.tree.map(lambda _: VMEM, out_shape)
    name = body.__name__.removesuffix("_body")
    return pl.pallas_call(
        body,
        name=name,
        out_shape=out_shape,
        in_specs=in_specs,
        out_specs=out_specs,
        compiler_params=pltpu.CompilerParams(vmem_limit_bytes=vmem * 1024 * 1024),
        cost_estimate=pl.CostEstimate(flops=COST.get(name, 1), bytes_accessed=1, transcendentals=0),
        **kwargs,
    )


def unit_body(here, img, txt, p, q, raw, sems):
    half = img.shape[0] // 2
    copies = []
    for j in range(2):
        part = pl.ds(j * half, half)
        for i, ref in enumerate((img, txt)):
            copies.append(
                pltpu.make_async_copy(ref.at[part], raw.at[i, part], sems.at[2 * j + i])
            )
    for copy in copies:
        copy.start()
    for j in range(2):
        part = pl.ds(j * half, half)
        unit = []
        for i in range(2):
            copies[2 * j + i].wait()
            values = raw[i, part].astype(jnp.float32)
            unit.append((values * inv_norm(values)).astype(jnp.bfloat16))

        @pl.when(here[0] < 2)
        def _():
            p[part] = unit[0]
            q[part] = unit[1]

        @pl.when(here[0] >= 2)
        def _():
            p[part] = unit[1]
            q[part] = unit[0]


def match_body(here, scale, shift, pos_far, sc, u_p, v_p, u_q, v_q, pos, sem):
    rows = u_p.shape[0]
    copy = pltpu.make_async_copy(pos_far, pos, sem)
    copy.start()
    sc[0:1] = jnp.full((1, sc.shape[1]), scale[0], jnp.float32)
    sc[1:2] = jnp.full((1, sc.shape[1]), shift[0], jnp.float32)
    me = here[0]
    lane = lax.broadcasted_iota(jnp.int32, (1, rows), 1)
    square = (rows, rows)
    diagonal = lax.broadcasted_iota(jnp.int32, square, 0) == lax.broadcasted_iota(
        jnp.int32, square, 1
    )

    def column(row):
        spread = jnp.where(diagonal, jnp.broadcast_to(row, square).astype(jnp.float32), 0.0)
        return jnp.sum(spread, axis=1, keepdims=True).astype(jnp.int32)

    copy.wait()
    blocks = [pos[:, k * rows : (k + 1) * rows] for k in range(4)]
    matches, places = [], []
    for j in range(4):
        them = me ^ j
        match = blocks[0]
        for k in range(1, 4):
            match = jnp.where(them == k, blocks[k], match)
        matches.append(match)
        places.append(them * rows + lane)

    def put(u_img, v_img, u_txt, v_txt):
        u_img[...] = column(matches[0])
        u_txt[...] = column(places[0])
        for j in range(4):
            v_img[j : j + 1] = places[j]
            v_txt[j : j + 1] = matches[j]

    @pl.when(me < 2)
    def _():
        put(u_p, v_p, u_q, v_q)

    @pl.when(me >= 2)
    def _():
        put(u_q, v_q, u_p, v_p)


def terms(x, ys, sc, positive=None):
    scale, shift = sc[0:1, 0:1], sc[1:2, 0:1]
    total = None
    for j, y in enumerate(ys):
        g = lax.logistic(scale * dot(x, y, NT) + shift)
        if positive is not None:
            u, v = positive
            g = g - (u == v[j]).astype(jnp.float32)
        term = dot((scale * g).astype(jnp.bfloat16), y, NN)
        total = term if total is None else total + term
    return total


def join_body(p, q, x2, y0, out):
    rows = p.shape[0]
    for j, part in enumerate((p, q, x2, y0)):
        out[j * rows : (j + 1) * rows] = part[...]


def own_body(sc, near, u_p, v_p, u_q, v_q, sum_p, sum_q):
    x, y, x2, y0 = (block(near, j) for j in range(4))
    sum_p[...] = terms(x, [y], sc, (u_p[...], [v_p[0:1]])) + terms(x, [y0], sc)
    sum_q[...] = terms(y, [x, x2], sc, (u_q[...], [v_q[0:1], v_q[2:3]]))


def take_body(y, _sum, out):
    out[...] = y[...]


def block(ref, j):
    rows = ref.shape[0] // 4
    return ref[j * rows : (j + 1) * rows]


def mid_body(sc, near, near_c, y1, part):
    part[...] = terms(block(near, 2), [block(near, 3), block(near_c, 3), y1[...]], sc)


def late_body(sc, near, y1_c, part, w2, out, w2_lo, w2_hi):
    half = w2_lo.shape[0]
    w2_lo[...] = w2[:half]
    w2_hi[...] = w2[half:]
    out[...] = (part[...] + terms(block(near, 2), [y1_c[...]], sc)).astype(out.dtype)


def tangent(raw, dunit):
    values = raw.astype(jnp.float32)
    inv = inv_norm(values)
    unit = values * inv
    return (dunit - unit * jnp.sum(unit * dunit, axis=-1, keepdims=True)) * inv


def write_out(is_txt, img, txt, dunit, img_grad, txt_grad, held, sems):
    def go(raw, grad):
        copies = []
        for j, (start, size) in enumerate(pieces_of(raw.shape[0])):
            part = pl.ds(start, size)
            held[part] = tangent(raw[part], dunit(part))
            copies.append(pltpu.make_async_copy(held.at[part], grad.at[part], sems.at[j]))
            copies[-1].start()
        for copy in copies:
            copy.wait()

    @pl.when(jnp.logical_not(is_txt))
    def _():
        go(img, img_grad)

    @pl.when(is_txt)
    def _():
        go(txt, txt_grad)


def visit_body(
    sc, near, near_c, y1, y1_c, w2, _send, u_p, v_p, u_q, v_q, own_p, own_q, sum_p, sum_q
):
    x, y = block(near, 0), block(near, 1)
    x_c, y_c, x2_c, y0_c = (block(near_c, j) for j in range(4))
    sum_p[...] = (
        own_p[...]
        + terms(x, [y_c, w2[...]], sc, (u_p[...], [v_p[1:2], v_p[2:3]]))
        + terms(x, [y0_c, y1[...], y1_c[...]], sc)
    )
    own = (u_q[...], [v_q[1:2], v_q[3:4]])
    sum_q[...] = own_q[...] + terms(y, [x_c, x2_c], sc, own)


def rest_body(
    sc, here, img, txt, p, w2_lo_c, w2_hi_c, u_p, v_p, sum_p, img_grad, txt_grad, total, held, sems
):
    half = p.shape[0] // 2
    own = (u_p[...], [v_p[3:4, :half], v_p[3:4, half:]])
    total[...] = sum_p[...] + terms(p[...], [w2_lo_c[...], w2_hi_c[...]], sc, own)
    write_out(here[0] >= 2, img, txt, lambda part: total[part], img_grad, txt_grad, held, sems)


def last_body(here, img, txt, sum_q, back, _img, _txt, img_grad, txt_grad, held, sems):
    def dunit(part):
        return sum_q[part] + back[part].astype(jnp.float32)

    write_out(here[0] < 2, img, txt, dunit, img_grad, txt_grad, held, sems)


def local(picture_vectors, caption_vectors, caption_position, sharpness_factor, affine_offset):
    groups = lax.axis_size("loop")
    rows, depth = picture_vectors.shape
    half = rows // 2
    img, txt, scale, shift = picture_vectors, caption_vectors, sharpness_factor, affine_offset

    def swap(to):
        pairs = []
        for g in range(groups):
            for n in range(4):
                h, m = to(g, n)
                pairs.append((g * 4 + n, (h % groups) * 4 + m))
        def go(x, name):
            with jax.named_scope(name):
                return lax.ppermute(x, AXES, pairs)

        return go

    core = swap(lambda g, n: (g, n ^ 1))
    chip = swap(lambda g, n: (g, n ^ 2))
    group = swap(lambda g, n: (g + 1, n - 2) if n >= 2 else (g - 1, n + 2))

    def of(shape, dtype=jnp.float32):
        return jax.ShapeDtypeStruct(shape, dtype)

    here = lax.axis_index("narrow").astype(jnp.int32).reshape(1)
    bf16 = jnp.bfloat16
    one, wide = of((rows, depth), bf16), of((rows, depth))
    part, four = of((half, depth), bf16), of((4 * rows, depth), bf16)
    dma = pltpu.SemaphoreType.DMA
    far = lambda x: pltpu.with_memory_space_constraint(x, pltpu.HBM)

    p, q = call(
        unit_body,
        (one, one),
        [SMEM, HBM, HBM],
        scratch_shapes=[pltpu.VMEM((2, rows, depth), bf16), dma((4,))],
    )(here, far(img), far(txt))
    x2 = chip(q, "chip_q")
    y0 = group(p, "group_p")
    y1 = group(x2, "group_x2")
    w2 = chip(p, "chip_p")

    place = (of((rows, 1), jnp.int32), of((4, rows), jnp.int32))
    sc, *match = call(
        match_body,
        (of((2, 128)),) + place + place,
        [SMEM] * 3 + [HBM],
        scratch_shapes=[pltpu.VMEM((1, 4 * rows), jnp.int32), dma],
    )(here, scale, shift, far(caption_position))
    near = call(join_body, four, [VMEM] * 4)(p, q, x2, y0)
    near_c = core(near, "core_xy")
    own_p, own_q = call(own_body, (wide, wide), [VMEM] * 6)(sc, near, *match)
    y1 = call(take_body, one, [VMEM] * 2)(y1, own_q)
    y1_c = core(y1, "core_y")
    part_x = call(mid_body, wide, [VMEM] * 4)(sc, near, near_c, y1)
    send, w2_lo, w2_hi = call(late_body, (one, part, part), [VMEM] * 5)(
        sc, near, y1_c, part_x, w2
    )
    back = chip(send, "chip_send")
    sum_p, sum_q = call(visit_body, (wide, wide), [VMEM] * 13)(
        sc, near, near_c, y1, y1_c, w2, send, *match, own_p, own_q
    )
    out = [pltpu.VMEM((rows, depth), jnp.float32), dma((4,))]
    grads = call(
        rest_body,
        (wide, wide),
        [VMEM, SMEM] + [VMEM] * 8,
        (HBM, HBM),
        scratch_shapes=[pltpu.VMEM((rows, depth), jnp.float32)] + out,
    )(sc, here, img, txt, p, core(w2_lo, "core_w_lo"), core(w2_hi, "core_w_hi"), *match[:2], sum_p)
    return call(
        last_body,
        (wide, wide),
        [SMEM] + [VMEM] * 4 + [HBM] * 2,
        (HBM, HBM),
        scratch_shapes=out,
        input_output_aliases={5: 0, 6: 1},
    )(here, img, txt, sum_q, back, *grads)


def solution(mesh):
    return jax.shard_map(
        local,
        mesh=mesh,
        in_specs=(
            P(AXES, None),
            P(AXES, None),
            P("loop", None),
            P(),
            P(),
        ),
        out_specs=(P(AXES, None), P(AXES, None)),
        check_vma=False,
    )
```

```python
import jax
import jax.numpy as jnp
from jax import lax
from jax.experimental import pallas as pl
from jax.experimental.pallas import tpu as pltpu
from jax.sharding import PartitionSpec as P

AXES = ("loop", "narrow")
VMEM = pl.BlockSpec(memory_space=pltpu.VMEM)
SMEM = pl.BlockSpec(memory_space=pltpu.SMEM)
HBM = pl.BlockSpec(memory_space=pltpu.HBM)
NT = (((1,), (1,)), ((), ()))
NN = (((1,), (0,)), ((), ()))
COST = {
    "unit": 16 * 10**9,
    "take": 64 * 10**9,
    "last": 64 * 10**9,
}


def pieces_of(rows):
    half = rows // 2
    first = half // 32 * 16
    edges = [0, first, half, half + first, rows]
    return [(low, high - low) for low, high in zip(edges, edges[1:])]


def inv_norm(values):
    return lax.rsqrt(jnp.sum(values * values, axis=-1, keepdims=True) + 1e-06)


def dot(a, b, dims):
    return lax.dot_general(a, b, dims, preferred_element_type=jnp.float32)


def call(body, out_shape, in_specs, out_specs=None, vmem=6, **kwargs):
    if out_specs is None:
        out_specs = jax.tree.map(lambda _: VMEM, out_shape)
    name = body.__name__.removesuffix("_body")
    return pl.pallas_call(
        body,
        name=name,
        out_shape=out_shape,
        in_specs=in_specs,
        out_specs=out_specs,
        compiler_params=pltpu.CompilerParams(vmem_limit_bytes=vmem * 1024 * 1024),
        cost_estimate=pl.CostEstimate(flops=COST.get(name, 1), bytes_accessed=1, transcendentals=0),
        **kwargs,
    )


def unit_body(here, img, txt, p, q, raw, sems):
    half = img.shape[0] // 2
    copies = []
    for j in range(2):
        part = pl.ds(j * half, half)
        for i, ref in enumerate((img, txt)):
            copies.append(
                pltpu.make_async_copy(ref.at[part], raw.at[i, part], sems.at[2 * j + i])
            )
    for copy in copies:
        copy.start()
    for j in range(2):
        part = pl.ds(j * half, half)
        unit = []
        for i in range(2):
            copies[2 * j + i].wait()
            values = raw[i, part].astype(jnp.float32)
            unit.append((values * inv_norm(values)).astype(jnp.bfloat16))

        @pl.when(here[0] < 2)
        def _():
            p[part] = unit[0]
            q[part] = unit[1]

        @pl.when(here[0] >= 2)
        def _():
            p[part] = unit[1]
            q[part] = unit[0]


def match_body(here, scale, shift, pos_far, sc, u_p, v_p, u_q, v_q, pos, sem):
    rows = u_p.shape[0]
    copy = pltpu.make_async_copy(pos_far, pos, sem)
    copy.start()
    sc[0:1] = jnp.full((1, sc.shape[1]), scale[0], jnp.float32)
    sc[1:2] = jnp.full((1, sc.shape[1]), shift[0], jnp.float32)
    me = here[0]
    lane = lax.broadcasted_iota(jnp.int32, (1, rows), 1)
    square = (rows, rows)
    diagonal = lax.broadcasted_iota(jnp.int32, square, 0) == lax.broadcasted_iota(
        jnp.int32, square, 1
    )

    def column(row):
        spread = jnp.where(diagonal, jnp.broadcast_to(row, square).astype(jnp.float32), 0.0)
        return jnp.sum(spread, axis=1, keepdims=True).astype(jnp.int32)

    copy.wait()
    blocks = [pos[:, k * rows : (k + 1) * rows] for k in range(4)]
    matches, places = [], []
    for j in range(4):
        them = me ^ j
        match = blocks[0]
        for k in range(1, 4):
            match = jnp.where(them == k, blocks[k], match)
        matches.append(match)
        places.append(them * rows + lane)

    def put(u_img, v_img, u_txt, v_txt):
        u_img[...] = column(matches[0])
        u_txt[...] = column(places[0])
        for j in range(4):
            v_img[j : j + 1] = places[j]
            v_txt[j : j + 1] = matches[j]

    @pl.when(me < 2)
    def _():
        put(u_p, v_p, u_q, v_q)

    @pl.when(me >= 2)
    def _():
        put(u_q, v_q, u_p, v_p)


def terms(x, ys, sc, positive=None):
    scale, shift = sc[0:1, 0:1], sc[1:2, 0:1]
    total = None
    for j, y in enumerate(ys):
        g = lax.logistic(scale * dot(x, y, NT) + shift)
        if positive is not None:
            u, v = positive
            g = g - (u == v[j]).astype(jnp.float32)
        term = dot((scale * g).astype(jnp.bfloat16), y, NN)
        total = term if total is None else total + term
    return total


def join_body(p, q, x2, y0, out):
    rows = p.shape[0]
    for j, part in enumerate((p, q, x2, y0)):
        out[j * rows : (j + 1) * rows] = part[...]


def own_body(sc, near, u_p, v_p, u_q, v_q, sum_p, sum_q):
    x, y, x2, y0 = (block(near, j) for j in range(4))
    sum_p[...] = terms(x, [y], sc, (u_p[...], [v_p[0:1]])) + terms(x, [y0], sc)
    sum_q[...] = terms(y, [x, x2], sc, (u_q[...], [v_q[0:1], v_q[2:3]]))


def take_body(y, _sum, out):
    out[...] = y[...]


def block(ref, j):
    rows = ref.shape[0] // 4
    return ref[j * rows : (j + 1) * rows]


def mid_body(sc, near, near_c, y1, part):
    part[...] = terms(block(near, 2), [block(near, 3), block(near_c, 3), y1[...]], sc)


def far_sums(sc, near, near_c, y1, y1_c, w2, u_p, v_p, u_q, v_q, own_p, own_q, sum_p, sum_q):
    x, y = block(near, 0), block(near, 1)
    x_c, y_c, x2_c, y0_c = (block(near_c, j) for j in range(4))
    sum_p[...] = (
        own_p[...]
        + terms(x, [y_c, w2[...]], sc, (u_p[...], [v_p[1:2], v_p[2:3]]))
        + terms(x, [y0_c, y1[...], y1_c[...]], sc)
    )
    own = (u_q[...], [v_q[1:2], v_q[3:4]])
    sum_q[...] = own_q[...] + terms(y, [x_c, x2_c], sc, own)


def late_body(here, part, sc, near, near_c, y1, y1_c, *rest):
    out, sum_p, sum_q = rest[-3:]

    @pl.when(here[0] % 2 == 0)
    def _():
        far_sums(sc, near, near_c, y1, y1_c, *rest[:-3], sum_p, sum_q)

    out[...] = (part[...] + terms(block(near, 2), [y1_c[...]], sc)).astype(out.dtype)


def tangent(raw, dunit):
    values = raw.astype(jnp.float32)
    inv = inv_norm(values)
    unit = values * inv
    return (dunit - unit * jnp.sum(unit * dunit, axis=-1, keepdims=True)) * inv


def write_out(is_txt, img, txt, dunit, img_grad, txt_grad, held, sems):
    def go(raw, grad):
        copies = []
        for j, (start, size) in enumerate(pieces_of(raw.shape[0])):
            part = pl.ds(start, size)
            held[part] = tangent(raw[part], dunit(part))
            copies.append(pltpu.make_async_copy(held.at[part], grad.at[part], sems.at[j]))
            copies[-1].start()
        for copy in copies:
            copy.wait()

    @pl.when(jnp.logical_not(is_txt))
    def _():
        go(img, img_grad)

    @pl.when(is_txt)
    def _():
        go(txt, txt_grad)


def visit_body(here, _send, _sum_p, _sum_q, sc, near, near_c, y1, y1_c, w2, *rest):
    sum_p, sum_q, w2_lo, w2_hi = rest[-4:]
    half = w2_lo.shape[0]
    w2_lo[...] = w2[:half]
    w2_hi[...] = w2[half:]

    @pl.when(here[0] % 2 == 1)
    def _():
        far_sums(sc, near, near_c, y1, y1_c, w2, *rest[:-4], sum_p, sum_q)


def rest_body(
    sc, here, img, txt, p, w2_lo_c, w2_hi_c, u_p, v_p, sum_p, img_grad, txt_grad, total, held, sems
):
    half = p.shape[0] // 2
    own = (u_p[...], [v_p[3:4, :half], v_p[3:4, half:]])
    total[...] = sum_p[...] + terms(p[...], [w2_lo_c[...], w2_hi_c[...]], sc, own)
    write_out(here[0] >= 2, img, txt, lambda part: total[part], img_grad, txt_grad, held, sems)


def last_body(here, img, txt, sum_q, back, _img, _txt, img_grad, txt_grad, held, sems):
    def dunit(part):
        return sum_q[part] + back[part].astype(jnp.float32)

    write_out(here[0] < 2, img, txt, dunit, img_grad, txt_grad, held, sems)


def local(picture_vectors, caption_vectors, caption_position, sharpness_factor, affine_offset):
    groups = lax.axis_size("loop")
    rows, depth = picture_vectors.shape
    half = rows // 2
    img, txt, scale, shift = picture_vectors, caption_vectors, sharpness_factor, affine_offset

    def swap(to):
        pairs = []
        for g in range(groups):
            for n in range(4):
                h, m = to(g, n)
                pairs.append((g * 4 + n, (h % groups) * 4 + m))
        def go(x, name):
            with jax.named_scope(name):
                return lax.ppermute(x, AXES, pairs)

        return go

    core = swap(lambda g, n: (g, n ^ 1))
    chip = swap(lambda g, n: (g, n ^ 2))
    group = swap(lambda g, n: (g + 1, n - 2) if n >= 2 else (g - 1, n + 2))

    def of(shape, dtype=jnp.float32):
        return jax.ShapeDtypeStruct(shape, dtype)

    here = lax.axis_index("narrow").astype(jnp.int32).reshape(1)
    bf16 = jnp.bfloat16
    one, wide = of((rows, depth), bf16), of((rows, depth))
    part, four = of((half, depth), bf16), of((4 * rows, depth), bf16)
    dma = pltpu.SemaphoreType.DMA
    far = lambda x: pltpu.with_memory_space_constraint(x, pltpu.HBM)

    p, q = call(
        unit_body,
        (one, one),
        [SMEM, HBM, HBM],
        scratch_shapes=[pltpu.VMEM((2, rows, depth), bf16), dma((4,))],
    )(here, far(img), far(txt))
    x2 = chip(q, "chip_q")
    y0 = group(p, "group_p")
    y1 = group(x2, "group_x2")
    w2 = chip(p, "chip_p")

    place = (of((rows, 1), jnp.int32), of((4, rows), jnp.int32))
    sc, *match = call(
        match_body,
        (of((2, 128)),) + place + place,
        [SMEM] * 3 + [HBM],
        scratch_shapes=[pltpu.VMEM((1, 4 * rows), jnp.int32), dma],
    )(here, scale, shift, far(caption_position))
    near = call(join_body, four, [VMEM] * 4)(p, q, x2, y0)
    near_c = core(near, "core_xy")
    own_p, own_q = call(own_body, (wide, wide), [VMEM] * 6)(sc, near, *match)
    y1 = call(take_body, one, [VMEM] * 2)(y1, own_q)
    y1_c = core(y1, "core_y")
    part_x = call(mid_body, wide, [VMEM] * 4)(sc, near, near_c, y1)
    blocks = (sc, near, near_c, y1, y1_c, w2, *match, own_p, own_q)
    send, sum_p, sum_q = call(late_body, (one, wide, wide), [SMEM] + [VMEM] * 13)(
        here, part_x, *blocks
    )
    back = chip(send, "chip_send")
    sum_p, sum_q, w2_lo, w2_hi = call(
        visit_body,
        (wide, wide, part, part),
        [SMEM] + [VMEM] * 15,
        input_output_aliases={2: 0, 3: 1},
    )(here, send, sum_p, sum_q, *blocks)
    out = [pltpu.VMEM((rows, depth), jnp.float32), dma((4,))]
    grads = call(
        rest_body,
        (wide, wide),
        [VMEM, SMEM] + [VMEM] * 8,
        (HBM, HBM),
        scratch_shapes=[pltpu.VMEM((rows, depth), jnp.float32)] + out,
    )(sc, here, img, txt, p, core(w2_lo, "core_w_lo"), core(w2_hi, "core_w_hi"), *match[:2], sum_p)
    return call(
        last_body,
        (wide, wide),
        [SMEM] + [VMEM] * 4 + [HBM] * 2,
        (HBM, HBM),
        scratch_shapes=out,
        input_output_aliases={5: 0, 6: 1},
    )(here, img, txt, sum_q, back, *grads)


def solution(mesh):
    return jax.shard_map(
        local,
        mesh=mesh,
        in_specs=(
            P(AXES, None),
            P(AXES, None),
            P("loop", None),
            P(),
            P(),
        ),
        out_specs=(P(AXES, None), P(AXES, None)),
        check_vma=False,
    )
```

```python
import jax
import jax.numpy as jnp
from jax import lax
from jax.experimental import pallas as pl
from jax.experimental.pallas import tpu as pltpu
from jax.sharding import PartitionSpec as P

AXES = ("loop", "narrow")
VMEM = pl.BlockSpec(memory_space=pltpu.VMEM)
SMEM = pl.BlockSpec(memory_space=pltpu.SMEM)
HBM = pl.BlockSpec(memory_space=pltpu.HBM)
NT = (((1,), (1,)), ((), ()))
NN = (((1,), (0,)), ((), ()))
COST = {"unit": 16 * 10**9, "take": 64 * 10**9, "last": 64 * 10**9, "nums": 10**9}


def pieces_of(rows):
    half = rows // 2
    first = half // 32 * 16
    edges = [0, first, half, half + first, rows]
    return [(low, high - low) for low, high in zip(edges, edges[1:])]


def inv_norm(values):
    return lax.rsqrt(jnp.sum(values * values, axis=-1, keepdims=True) + 1e-06)


def dot(a, b, dims):
    return lax.dot_general(a, b, dims, preferred_element_type=jnp.float32)


def call(body, out_shape, in_specs, out_specs=None, vmem=6, **kwargs):
    if out_specs is None:
        out_specs = jax.tree.map(lambda _: VMEM, out_shape)
    name = body.__name__.removesuffix("_body")
    return pl.pallas_call(
        body,
        name=name,
        out_shape=out_shape,
        in_specs=in_specs,
        out_specs=out_specs,
        compiler_params=pltpu.CompilerParams(vmem_limit_bytes=vmem * 1024 * 1024),
        cost_estimate=pl.CostEstimate(flops=COST.get(name, 1), bytes_accessed=1, transcendentals=0),
        **kwargs,
    )


def unit_body(here, img, txt, pos_far, p, q, *rest):
    raw, sems = rest[-2:]
    half = img.shape[0] // 2
    copies = []
    for j in range(2):
        part = pl.ds(j * half, half)
        for i, ref in enumerate((img, txt)):
            copies.append(
                pltpu.make_async_copy(ref.at[part], raw.at[i, part], sems.at[2 * j + i])
            )
    for copy in copies:
        copy.start()
    for j in range(2):
        part = pl.ds(j * half, half)
        unit = []
        for i in range(2):
            copies[2 * j + i].wait()
            values = raw[i, part].astype(jnp.float32)
            unit.append((values * inv_norm(values)).astype(jnp.bfloat16))

        @pl.when(here[0] < 2)
        def _():
            p[part] = unit[0]
            q[part] = unit[1]

        @pl.when(here[0] >= 2)
        def _():
            p[part] = unit[1]
            q[part] = unit[0]

    @pl.when(here[0] % 2 == 0)
    def _():
        spots(here, pos_far, *rest[:-2])


def nums_body(scale, shift, sc):
    sc[0:1] = jnp.full((1, sc.shape[1]), scale[0], jnp.float32)
    sc[1:2] = jnp.full((1, sc.shape[1]), shift[0], jnp.float32)


def match_body(here, pos_far, *rest):
    @pl.when(here[0] % 2 == 1)
    def _():
        spots(here, pos_far, *rest[4:])


def spots(here, pos_far, u_p, v_p, u_q, v_q, pos, sem):
    rows = u_p.shape[0]
    copy = pltpu.make_async_copy(pos_far, pos, sem)
    copy.start()
    copy.wait()
    me = here[0]
    lane = lax.broadcasted_iota(jnp.int32, (1, rows), 1)
    square = (rows, rows)
    diagonal = lax.broadcasted_iota(jnp.int32, square, 0) == lax.broadcasted_iota(
        jnp.int32, square, 1
    )

    def column(row):
        spread = jnp.where(diagonal, jnp.broadcast_to(row, square).astype(jnp.float32), 0.0)
        return jnp.sum(spread, axis=1, keepdims=True).astype(jnp.int32)

    blocks = [pos[:, k * rows : (k + 1) * rows] for k in range(4)]
    matches, places = [], []
    for j in range(4):
        them = me ^ j
        match = blocks[0]
        for k in range(1, 4):
            match = jnp.where(them == k, blocks[k], match)
        matches.append(match)
        places.append(them * rows + lane)

    def put(u_img, v_img, u_txt, v_txt):
        u_img[...] = column(matches[0])
        u_txt[...] = column(places[0])
        for j in range(4):
            v_img[j : j + 1] = places[j]
            v_txt[j : j + 1] = matches[j]

    @pl.when(me < 2)
    def _():
        put(u_p, v_p, u_q, v_q)

    @pl.when(me >= 2)
    def _():
        put(u_q, v_q, u_p, v_p)


def terms(x, ys, sc, positive=None):
    scale, shift = sc[0:1, 0:1], sc[1:2, 0:1]
    total = None
    for j, y in enumerate(ys):
        g = lax.logistic(scale * dot(x, y, NT) + shift)
        if positive is not None:
            u, v = positive
            g = g - (u == v[j]).astype(jnp.float32)
        term = dot((scale * g).astype(jnp.bfloat16), y, NN)
        total = term if total is None else total + term
    return total


def join_body(p, q, x2, y0, out):
    rows = p.shape[0]
    for j, part in enumerate((p, q, x2, y0)):
        out[j * rows : (j + 1) * rows] = part[...]


def own_body(sc, near, u_p, v_p, u_q, v_q, sum_p, sum_q):
    x, y, x2, y0 = (block(near, j) for j in range(4))
    sum_p[...] = terms(x, [y], sc, (u_p[...], [v_p[0:1]])) + terms(x, [y0], sc)
    sum_q[...] = terms(y, [x, x2], sc, (u_q[...], [v_q[0:1], v_q[2:3]]))


def take_body(y, _sum, out):
    out[...] = y[...]


def block(ref, j):
    rows = ref.shape[0] // 4
    return ref[j * rows : (j + 1) * rows]


def mid_body(sc, near, near_c, y1, part):
    part[...] = terms(block(near, 2), [block(near, 3), block(near_c, 3), y1[...]], sc)


def far_sums(sc, near, near_c, y1, y1_c, w2, u_p, v_p, u_q, v_q, own_p, own_q, sum_p, sum_q):
    x, y = block(near, 0), block(near, 1)
    x_c, y_c, x2_c, y0_c = (block(near_c, j) for j in range(4))
    sum_p[...] = (
        own_p[...]
        + terms(x, [y_c, w2[...]], sc, (u_p[...], [v_p[1:2], v_p[2:3]]))
        + terms(x, [y0_c, y1[...], y1_c[...]], sc)
    )
    own = (u_q[...], [v_q[1:2], v_q[3:4]])
    sum_q[...] = own_q[...] + terms(y, [x_c, x2_c], sc, own)


def late_body(here, part, sc, near, near_c, y1, y1_c, *rest):
    out, sum_p, sum_q = rest[-3:]

    @pl.when(here[0] % 2 == 0)
    def _():
        far_sums(sc, near, near_c, y1, y1_c, *rest[:-3], sum_p, sum_q)

    out[...] = (part[...] + terms(block(near, 2), [y1_c[...]], sc)).astype(out.dtype)


def tangent(raw, dunit):
    values = raw.astype(jnp.float32)
    inv = inv_norm(values)
    unit = values * inv
    return (dunit - unit * jnp.sum(unit * dunit, axis=-1, keepdims=True)) * inv


def write_out(is_txt, img, txt, dunit, img_grad, txt_grad, held, sems):
    def go(raw, grad):
        copies = []
        for j, (start, size) in enumerate(pieces_of(raw.shape[0])):
            part = pl.ds(start, size)
            held[part] = tangent(raw[part], dunit(part))
            copies.append(pltpu.make_async_copy(held.at[part], grad.at[part], sems.at[j]))
            copies[-1].start()
        for copy in copies:
            copy.wait()

    @pl.when(jnp.logical_not(is_txt))
    def _():
        go(img, img_grad)

    @pl.when(is_txt)
    def _():
        go(txt, txt_grad)


def visit_body(here, _send, _sum_p, _sum_q, sc, near, near_c, y1, y1_c, w2, *rest):
    sum_p, sum_q, w2_lo, w2_hi = rest[-4:]
    half = w2_lo.shape[0]
    w2_lo[...] = w2[:half]
    w2_hi[...] = w2[half:]

    @pl.when(here[0] % 2 == 1)
    def _():
        far_sums(sc, near, near_c, y1, y1_c, w2, *rest[:-4], sum_p, sum_q)


def rest_body(
    sc, here, img, txt, p, w2_lo_c, w2_hi_c, u_p, v_p, sum_p, img_grad, txt_grad, total, held, sems
):
    half = p.shape[0] // 2
    own = (u_p[...], [v_p[3:4, :half], v_p[3:4, half:]])
    total[...] = sum_p[...] + terms(p[...], [w2_lo_c[...], w2_hi_c[...]], sc, own)
    write_out(here[0] >= 2, img, txt, lambda part: total[part], img_grad, txt_grad, held, sems)


def last_body(here, img, txt, sum_q, back, _img, _txt, img_grad, txt_grad, held, sems):
    def dunit(part):
        return sum_q[part] + back[part].astype(jnp.float32)

    write_out(here[0] < 2, img, txt, dunit, img_grad, txt_grad, held, sems)


def local(picture_vectors, caption_vectors, caption_position, sharpness_factor, affine_offset):
    groups = lax.axis_size("loop")
    rows, depth = picture_vectors.shape
    half = rows // 2
    img, txt, scale, shift = picture_vectors, caption_vectors, sharpness_factor, affine_offset

    def swap(to):
        pairs = []
        for g in range(groups):
            for n in range(4):
                h, m = to(g, n)
                pairs.append((g * 4 + n, (h % groups) * 4 + m))
        def go(x, name):
            with jax.named_scope(name):
                return lax.ppermute(x, AXES, pairs)

        return go

    core = swap(lambda g, n: (g, n ^ 1))
    chip = swap(lambda g, n: (g, n ^ 2))
    group = swap(lambda g, n: (g + 1, n - 2) if n >= 2 else (g - 1, n + 2))

    def of(shape, dtype=jnp.float32):
        return jax.ShapeDtypeStruct(shape, dtype)

    here = lax.axis_index("narrow").astype(jnp.int32).reshape(1)
    bf16 = jnp.bfloat16
    one, wide = of((rows, depth), bf16), of((rows, depth))
    part, four = of((half, depth), bf16), of((4 * rows, depth), bf16)
    dma = pltpu.SemaphoreType.DMA
    far = lambda x: pltpu.with_memory_space_constraint(x, pltpu.HBM)

    place = (of((rows, 1), jnp.int32), of((4, rows), jnp.int32)) * 2
    pos = far(caption_position)
    reading = [pltpu.VMEM((1, 4 * rows), jnp.int32), dma]
    p, q, *spot = call(
        unit_body,
        (one, one) + place,
        [SMEM] + [HBM] * 3,
        scratch_shapes=reading + [pltpu.VMEM((2, rows, depth), bf16), dma((4,))],
    )(here, far(img), far(txt), pos)
    x2 = chip(q, "chip_q")
    y0 = group(p, "group_p")
    y1 = group(x2, "group_x2")
    w2 = chip(p, "chip_p")

    sc = call(nums_body, of((2, 128)), [SMEM] * 2)(scale, shift)
    match = call(
        match_body,
        place,
        [SMEM, HBM] + [VMEM] * 4,
        scratch_shapes=reading,
        input_output_aliases={2 + j: j for j in range(4)},
    )(here, pos, *spot)
    near = call(join_body, four, [VMEM] * 4)(p, q, x2, y0)
    near_c = core(near, "core_xy")
    own_p, own_q = call(own_body, (wide, wide), [VMEM] * 6)(sc, near, *match)
    y1 = call(take_body, one, [VMEM] * 2)(y1, own_q)
    y1_c = core(y1, "core_y")
    part_x = call(mid_body, wide, [VMEM] * 4)(sc, near, near_c, y1)
    blocks = (sc, near, near_c, y1, y1_c, w2, *match, own_p, own_q)
    send, sum_p, sum_q = call(late_body, (one, wide, wide), [SMEM] + [VMEM] * 13)(
        here, part_x, *blocks
    )
    back = chip(send, "chip_send")
    sum_p, sum_q, w2_lo, w2_hi = call(
        visit_body,
        (wide, wide, part, part),
        [SMEM] + [VMEM] * 15,
        input_output_aliases={2: 0, 3: 1},
    )(here, send, sum_p, sum_q, *blocks)
    out = [pltpu.VMEM((rows, depth), jnp.float32), dma((4,))]
    grads = call(
        rest_body,
        (wide, wide),
        [VMEM, SMEM] + [VMEM] * 8,
        (HBM, HBM),
        scratch_shapes=[pltpu.VMEM((rows, depth), jnp.float32)] + out,
    )(sc, here, img, txt, p, core(w2_lo, "core_w_lo"), core(w2_hi, "core_w_hi"), *match[:2], sum_p)
    return call(
        last_body,
        (wide, wide),
        [SMEM] + [VMEM] * 4 + [HBM] * 2,
        (HBM, HBM),
        scratch_shapes=out,
        input_output_aliases={5: 0, 6: 1},
    )(here, img, txt, sum_q, back, *grads)


def solution(mesh):
    return jax.shard_map(
        local,
        mesh=mesh,
        in_specs=(
            P(AXES, None),
            P(AXES, None),
            P("loop", None),
            P(),
            P(),
        ),
        out_specs=(P(AXES, None), P(AXES, None)),
        check_vma=False,
    )
```

```python
import jax
import jax.numpy as jnp
from jax import lax
from jax.experimental import pallas as pl
from jax.experimental.pallas import tpu as pltpu
from jax.sharding import PartitionSpec as P

AXES = ("loop", "narrow")
VMEM = pl.BlockSpec(memory_space=pltpu.VMEM)
SMEM = pl.BlockSpec(memory_space=pltpu.SMEM)
HBM = pl.BlockSpec(memory_space=pltpu.HBM)
NT = (((1,), (1,)), ((), ()))
NN = (((1,), (0,)), ((), ()))
COST = {"unit": 16 * 10**9, "take": 64 * 10**9, "last": 64 * 10**9, "nums": 10**9}


def pieces_of(rows):
    half = rows // 2
    first = half // 32 * 16
    edges = [0, first, half, half + first, rows]
    return [(low, high - low) for low, high in zip(edges, edges[1:])]


def inv_norm(values):
    return lax.rsqrt(jnp.sum(values * values, axis=-1, keepdims=True) + 1e-06)


def dot(a, b, dims):
    return lax.dot_general(a, b, dims, preferred_element_type=jnp.float32)


def call(body, out_shape, in_specs, out_specs=None, vmem=6, **kwargs):
    if out_specs is None:
        out_specs = jax.tree.map(lambda _: VMEM, out_shape)
    name = body.__name__.removesuffix("_body")
    return pl.pallas_call(
        body,
        name=name,
        out_shape=out_shape,
        in_specs=in_specs,
        out_specs=out_specs,
        compiler_params=pltpu.CompilerParams(vmem_limit_bytes=vmem * 1024 * 1024),
        cost_estimate=pl.CostEstimate(flops=COST.get(name, 1), bytes_accessed=1, transcendentals=0),
        **kwargs,
    )


def unit_body(here, img, txt, pos_far, p, q, *rest):
    raw, sems = rest[-2:]
    copies = []
    for i, ref in enumerate((img, txt)):
        copies.append(pltpu.make_async_copy(ref, raw.at[i], sems.at[i]))
        copies[-1].start()

    def unit(i):
        copies[i].wait()
        values = raw[i].astype(jnp.float32)
        return (values * inv_norm(values)).astype(jnp.bfloat16)

    @pl.when(here[0] < 2)
    def _():
        p[...] = unit(0)
        q[...] = unit(1)

    @pl.when(here[0] >= 2)
    def _():
        p[...] = unit(1)
        q[...] = unit(0)

    @pl.when(here[0] % 2 == 0)
    def _():
        spots(here, pos_far, *rest[:-2])


def nums_body(scale, shift, sc):
    sc[0:1] = jnp.full((1, sc.shape[1]), scale[0], jnp.float32)
    sc[1:2] = jnp.full((1, sc.shape[1]), shift[0], jnp.float32)


def match_body(here, pos_far, *rest):
    @pl.when(here[0] % 2 == 1)
    def _():
        spots(here, pos_far, *rest[4:])


def spots(here, pos_far, u_p, v_p, u_q, v_q, pos, sem):
    rows = u_p.shape[0]
    copy = pltpu.make_async_copy(pos_far, pos, sem)
    copy.start()
    copy.wait()
    me = here[0]
    lane = lax.broadcasted_iota(jnp.int32, (1, rows), 1)
    square = (rows, rows)
    diagonal = lax.broadcasted_iota(jnp.int32, square, 0) == lax.broadcasted_iota(
        jnp.int32, square, 1
    )

    def column(row):
        spread = jnp.where(diagonal, jnp.broadcast_to(row, square).astype(jnp.float32), 0.0)
        return jnp.sum(spread, axis=1, keepdims=True).astype(jnp.int32)

    blocks = [pos[:, k * rows : (k + 1) * rows] for k in range(4)]
    matches, places = [], []
    for j in range(4):
        them = me ^ j
        match = blocks[0]
        for k in range(1, 4):
            match = jnp.where(them == k, blocks[k], match)
        matches.append(match)
        places.append(them * rows + lane)

    def put(u_img, v_img, u_txt, v_txt):
        u_img[...] = column(matches[0])
        u_txt[...] = column(places[0])
        for j in range(4):
            v_img[j : j + 1] = places[j]
            v_txt[j : j + 1] = matches[j]

    @pl.when(me < 2)
    def _():
        put(u_p, v_p, u_q, v_q)

    @pl.when(me >= 2)
    def _():
        put(u_q, v_q, u_p, v_p)


def terms(x, ys, sc, positive=None):
    scale, shift = sc[0:1, 0:1], sc[1:2, 0:1]
    total = None
    for j, y in enumerate(ys):
        g = lax.logistic(scale * dot(x, y, NT) + shift)
        if positive is not None:
            u, v = positive
            g = g - (u == v[j]).astype(jnp.float32)
        term = dot((scale * g).astype(jnp.bfloat16), y, NN)
        total = term if total is None else total + term
    return total


def join_body(p, q, x2, y0, out):
    rows = p.shape[0]
    for j, part in enumerate((p, q, x2, y0)):
        out[j * rows : (j + 1) * rows] = part[...]


def own_body(sc, near, u_p, v_p, u_q, v_q, sum_p, sum_q, part):
    x, y, x2, y0 = (block(near, j) for j in range(4))
    part[...] = terms(x2, [y0], sc)
    sum_p[...] = terms(x, [y], sc, (u_p[...], [v_p[0:1]])) + terms(x, [y0], sc)
    sum_q[...] = terms(y, [x, x2], sc, (u_q[...], [v_q[0:1], v_q[2:3]]))


def take_body(y, _sum, out):
    out[...] = y[...]


def block(ref, j):
    rows = ref.shape[0] // 4
    return ref[j * rows : (j + 1) * rows]


def mid_body(sc, near, near_c, y1, part, out):
    out[...] = part[...] + terms(block(near, 2), [block(near_c, 3), y1[...]], sc)


def far_sums(sc, near, near_c, y1, y1_c, w2, u_p, v_p, u_q, v_q, own_p, own_q, sum_p, sum_q):
    x, y = block(near, 0), block(near, 1)
    x_c, y_c, x2_c, y0_c = (block(near_c, j) for j in range(4))
    sum_p[...] = (
        own_p[...]
        + terms(x, [y_c, w2[...]], sc, (u_p[...], [v_p[1:2], v_p[2:3]]))
        + terms(x, [y0_c, y1[...], y1_c[...]], sc)
    )
    own = (u_q[...], [v_q[1:2], v_q[3:4]])
    sum_q[...] = own_q[...] + terms(y, [x_c, x2_c], sc, own)


def late_body(here, part, sc, near, near_c, y1, y1_c, *rest):
    out, sum_p, sum_q = rest[-3:]

    @pl.when(here[0] % 2 == 0)
    def _():
        far_sums(sc, near, near_c, y1, y1_c, *rest[:-3], sum_p, sum_q)

    out[...] = (part[...] + terms(block(near, 2), [y1_c[...]], sc)).astype(out.dtype)


def tangent(raw, dunit):
    values = raw.astype(jnp.float32)
    inv = inv_norm(values)
    unit = values * inv
    return (dunit - unit * jnp.sum(unit * dunit, axis=-1, keepdims=True)) * inv


def write_out(is_txt, img, txt, dunit, img_grad, txt_grad, held, sems):
    def go(raw, grad):
        copies = []
        for j, (start, size) in enumerate(pieces_of(raw.shape[0])):
            part = pl.ds(start, size)
            held[part] = tangent(raw[part], dunit(part))
            copies.append(pltpu.make_async_copy(held.at[part], grad.at[part], sems.at[j]))
            copies[-1].start()
        for copy in copies:
            copy.wait()

    @pl.when(jnp.logical_not(is_txt))
    def _():
        go(img, img_grad)

    @pl.when(is_txt)
    def _():
        go(txt, txt_grad)


def visit_body(here, _send, _sum_p, _sum_q, sc, near, near_c, y1, y1_c, w2, *rest):
    sum_p, sum_q, w2_lo, w2_hi = rest[-4:]
    half = w2_lo.shape[0]
    w2_lo[...] = w2[:half]
    w2_hi[...] = w2[half:]

    @pl.when(here[0] % 2 == 1)
    def _():
        far_sums(sc, near, near_c, y1, y1_c, w2, *rest[:-4], sum_p, sum_q)


def rest_body(
    sc, here, img, txt, p, w2_lo_c, w2_hi_c, u_p, v_p, sum_p, img_grad, txt_grad, total, held, sems
):
    half = p.shape[0] // 2
    own = (u_p[...], [v_p[3:4, :half], v_p[3:4, half:]])
    total[...] = sum_p[...] + terms(p[...], [w2_lo_c[...], w2_hi_c[...]], sc, own)
    write_out(here[0] >= 2, img, txt, lambda part: total[part], img_grad, txt_grad, held, sems)


def last_body(here, img, txt, sum_q, back, _img, _txt, img_grad, txt_grad, held, sems):
    def dunit(part):
        return sum_q[part] + back[part].astype(jnp.float32)

    write_out(here[0] < 2, img, txt, dunit, img_grad, txt_grad, held, sems)


def local(picture_vectors, caption_vectors, caption_position, sharpness_factor, affine_offset):
    groups = lax.axis_size("loop")
    rows, depth = picture_vectors.shape
    half = rows // 2
    img, txt, scale, shift = picture_vectors, caption_vectors, sharpness_factor, affine_offset

    def swap(to):
        pairs = []
        for g in range(groups):
            for n in range(4):
                h, m = to(g, n)
                pairs.append((g * 4 + n, (h % groups) * 4 + m))
        def go(x, name):
            with jax.named_scope(name):
                return lax.ppermute(x, AXES, pairs)

        return go

    core = swap(lambda g, n: (g, n ^ 1))
    chip = swap(lambda g, n: (g, n ^ 2))
    group = swap(lambda g, n: (g + 1, n - 2) if n >= 2 else (g - 1, n + 2))

    def of(shape, dtype=jnp.float32):
        return jax.ShapeDtypeStruct(shape, dtype)

    here = lax.axis_index("narrow").astype(jnp.int32).reshape(1)
    bf16 = jnp.bfloat16
    one, wide = of((rows, depth), bf16), of((rows, depth))
    part, four = of((half, depth), bf16), of((4 * rows, depth), bf16)
    dma = pltpu.SemaphoreType.DMA
    far = lambda x: pltpu.with_memory_space_constraint(x, pltpu.HBM)

    place = (of((rows, 1), jnp.int32), of((4, rows), jnp.int32)) * 2
    pos = far(caption_position)
    reading = [pltpu.VMEM((1, 4 * rows), jnp.int32), dma]
    p, q, *spot = call(
        unit_body,
        (one, one) + place,
        [SMEM] + [HBM] * 3,
        scratch_shapes=reading + [pltpu.VMEM((2, rows, depth), bf16), dma((2,))],
    )(here, far(img), far(txt), pos)
    x2 = chip(q, "chip_q")
    y0 = group(p, "group_p")
    y1 = group(x2, "group_x2")
    w2 = chip(p, "chip_p")

    sc = call(nums_body, of((2, 128)), [SMEM] * 2)(scale, shift)
    match = call(
        match_body,
        place,
        [SMEM, HBM] + [VMEM] * 4,
        scratch_shapes=reading,
        input_output_aliases={2 + j: j for j in range(4)},
    )(here, pos, *spot)
    near = call(join_body, four, [VMEM] * 4)(p, q, x2, y0)
    near_c = core(near, "core_xy")
    own_p, own_q, part_x = call(own_body, (wide,) * 3, [VMEM] * 6)(sc, near, *match)
    y1 = call(take_body, one, [VMEM] * 2)(y1, own_q)
    y1_c = core(y1, "core_y")
    part_x = call(mid_body, wide, [VMEM] * 5)(sc, near, near_c, y1, part_x)
    blocks = (sc, near, near_c, y1, y1_c, w2, *match, own_p, own_q)
    send, sum_p, sum_q = call(late_body, (one, wide, wide), [SMEM] + [VMEM] * 13)(
        here, part_x, *blocks
    )
    back = chip(send, "chip_send")
    sum_p, sum_q, w2_lo, w2_hi = call(
        visit_body,
        (wide, wide, part, part),
        [SMEM] + [VMEM] * 15,
        input_output_aliases={2: 0, 3: 1},
    )(here, send, sum_p, sum_q, *blocks)
    out = [pltpu.VMEM((rows, depth), jnp.float32), dma((4,))]
    grads = call(
        rest_body,
        (wide, wide),
        [VMEM, SMEM] + [VMEM] * 8,
        (HBM, HBM),
        scratch_shapes=[pltpu.VMEM((rows, depth), jnp.float32)] + out,
    )(sc, here, img, txt, p, core(w2_lo, "core_w_lo"), core(w2_hi, "core_w_hi"), *match[:2], sum_p)
    return call(
        last_body,
        (wide, wide),
        [SMEM] + [VMEM] * 4 + [HBM] * 2,
        (HBM, HBM),
        scratch_shapes=out,
        input_output_aliases={5: 0, 6: 1},
    )(here, img, txt, sum_q, back, *grads)


def solution(mesh):
    return jax.shard_map(
        local,
        mesh=mesh,
        in_specs=(
            P(AXES, None),
            P(AXES, None),
            P("loop", None),
            P(),
            P(),
        ),
        out_specs=(P(AXES, None), P(AXES, None)),
        check_vma=False,
    )
```

```python
import jax
import jax.numpy as jnp
from jax import lax
from jax.experimental import pallas as pl
from jax.experimental.pallas import tpu as pltpu
from jax.sharding import PartitionSpec as P

AXES = ("loop", "narrow")
VMEM = pl.BlockSpec(memory_space=pltpu.VMEM)
SMEM = pl.BlockSpec(memory_space=pltpu.SMEM)
HBM = pl.BlockSpec(memory_space=pltpu.HBM)
NT = (((1,), (1,)), ((), ()))
NN = (((1,), (0,)), ((), ()))
COST = {"unit": 16 * 10**9, "take": 64 * 10**9, "last": 64 * 10**9, "nums": 10**9}


def pieces_of(rows):
    half = rows // 2
    first = half // 32 * 16
    edges = [0, first, half, half + first, rows]
    return [(low, high - low) for low, high in zip(edges, edges[1:])]


def inv_norm(values):
    return lax.rsqrt(jnp.sum(values * values, axis=-1, keepdims=True) + 1e-06)


def dot(a, b, dims):
    return lax.dot_general(a, b, dims, preferred_element_type=jnp.float32)


def call(body, out_shape, in_specs, out_specs=None, vmem=6, **kwargs):
    if out_specs is None:
        out_specs = jax.tree.map(lambda _: VMEM, out_shape)
    name = body.__name__.removesuffix("_body")
    return pl.pallas_call(
        body,
        name=name,
        out_shape=out_shape,
        in_specs=in_specs,
        out_specs=out_specs,
        compiler_params=pltpu.CompilerParams(vmem_limit_bytes=vmem * 1024 * 1024),
        cost_estimate=pl.CostEstimate(flops=COST.get(name, 1), bytes_accessed=1, transcendentals=0),
        **kwargs,
    )


def unit_body(here, img, txt, pos_far, p, q, *rest):
    raw, sems = rest[-2:]
    copies = []
    for i, ref in enumerate((img, txt)):
        copies.append(pltpu.make_async_copy(ref, raw.at[i], sems.at[i]))
        copies[-1].start()

    def unit(i):
        copies[i].wait()
        values = raw[i].astype(jnp.float32)
        return (values * inv_norm(values)).astype(jnp.bfloat16)

    @pl.when(here[0] < 2)
    def _():
        p[...] = unit(0)
        q[...] = unit(1)

    @pl.when(here[0] >= 2)
    def _():
        p[...] = unit(1)
        q[...] = unit(0)

    @pl.when(here[0] % 2 == 0)
    def _():
        spots(here, pos_far, *rest[:-2])


def nums_body(scale, shift, sc):
    sc[0:1] = jnp.full((1, sc.shape[1]), scale[0], jnp.float32)
    sc[1:2] = jnp.full((1, sc.shape[1]), shift[0], jnp.float32)


def match_body(here, pos_far, *rest):
    @pl.when(here[0] % 2 == 1)
    def _():
        spots(here, pos_far, *rest[4:])


def spots(here, pos_far, u_p, v_p, u_q, v_q, pos, sem):
    rows = u_p.shape[0]
    copy = pltpu.make_async_copy(pos_far, pos, sem)
    copy.start()
    copy.wait()
    me = here[0]
    lane = lax.broadcasted_iota(jnp.int32, (1, rows), 1)
    square = (rows, rows)
    diagonal = lax.broadcasted_iota(jnp.int32, square, 0) == lax.broadcasted_iota(
        jnp.int32, square, 1
    )

    def column(row):
        spread = jnp.where(diagonal, jnp.broadcast_to(row, square).astype(jnp.float32), 0.0)
        return jnp.sum(spread, axis=1, keepdims=True).astype(jnp.int32)

    blocks = [pos[:, k * rows : (k + 1) * rows] for k in range(4)]
    matches, places = [], []
    for j in range(4):
        them = me ^ j
        match = blocks[0]
        for k in range(1, 4):
            match = jnp.where(them == k, blocks[k], match)
        matches.append(match)
        places.append(them * rows + lane)

    def put(u_img, v_img, u_txt, v_txt):
        u_img[...] = column(matches[0])
        u_txt[...] = column(places[0])
        for j in range(4):
            v_img[j : j + 1] = places[j]
            v_txt[j : j + 1] = matches[j]

    @pl.when(me < 2)
    def _():
        put(u_p, v_p, u_q, v_q)

    @pl.when(me >= 2)
    def _():
        put(u_q, v_q, u_p, v_p)


def terms(x, ys, sc, positive=None):
    scale, shift = sc[0:1, 0:1], sc[1:2, 0:1]
    logits = [scale * dot(x, y, NT) + shift for y in ys]
    weights = []
    for j, logit in enumerate(logits):
        g = lax.logistic(logit)
        if positive is not None:
            u, v = positive
            g = g - (u == v[j]).astype(jnp.float32)
        weights.append((scale * g).astype(jnp.bfloat16))
    total = None
    for g, y in zip(weights, ys):
        term = dot(g, y, NN)
        total = term if total is None else total + term
    return total


def join_body(p, q, x2, y0, out):
    rows = p.shape[0]
    for j, part in enumerate((p, q, x2, y0)):
        out[j * rows : (j + 1) * rows] = part[...]


def own_body(sc, near, u_p, v_p, u_q, v_q, sum_p, sum_q, part):
    x, y, x2, y0 = (block(near, j) for j in range(4))
    part[...] = terms(x2, [y0], sc)
    sum_p[...] = terms(x, [y], sc, (u_p[...], [v_p[0:1]])) + terms(x, [y0], sc)
    sum_q[...] = terms(y, [x, x2], sc, (u_q[...], [v_q[0:1], v_q[2:3]]))


def take_body(y, _sum, out):
    out[...] = y[...]


def block(ref, j):
    rows = ref.shape[0] // 4
    return ref[j * rows : (j + 1) * rows]


def mid_body(sc, near, near_c, y1, part, out):
    out[...] = part[...] + terms(block(near, 2), [block(near_c, 3), y1[...]], sc)


def far_sums(sc, near, near_c, y1, y1_c, w2, u_p, v_p, u_q, v_q, own_p, own_q, sum_p, sum_q):
    x, y = block(near, 0), block(near, 1)
    x_c, y_c, x2_c, y0_c = (block(near_c, j) for j in range(4))
    sum_p[...] = (
        own_p[...]
        + terms(x, [y_c, w2[...]], sc, (u_p[...], [v_p[1:2], v_p[2:3]]))
        + terms(x, [y0_c, y1[...], y1_c[...]], sc)
    )
    own = (u_q[...], [v_q[1:2], v_q[3:4]])
    sum_q[...] = own_q[...] + terms(y, [x_c, x2_c], sc, own)


def late_body(here, part, sc, near, near_c, y1, y1_c, *rest):
    out, sum_p, sum_q = rest[-3:]

    @pl.when(here[0] % 2 == 0)
    def _():
        far_sums(sc, near, near_c, y1, y1_c, *rest[:-3], sum_p, sum_q)

    out[...] = (part[...] + terms(block(near, 2), [y1_c[...]], sc)).astype(out.dtype)


def tangent(raw, dunit):
    values = raw.astype(jnp.float32)
    inv = inv_norm(values)
    unit = values * inv
    return (dunit - unit * jnp.sum(unit * dunit, axis=-1, keepdims=True)) * inv


def write_out(is_txt, img, txt, dunit, img_grad, txt_grad, held, sems):
    def go(raw, grad):
        copies = []
        for j, (start, size) in enumerate(pieces_of(raw.shape[0])):
            part = pl.ds(start, size)
            held[part] = tangent(raw[part], dunit(part))
            copies.append(pltpu.make_async_copy(held.at[part], grad.at[part], sems.at[j]))
            copies[-1].start()
        for copy in copies:
            copy.wait()

    @pl.when(jnp.logical_not(is_txt))
    def _():
        go(img, img_grad)

    @pl.when(is_txt)
    def _():
        go(txt, txt_grad)


def visit_body(here, _send, _sum_p, _sum_q, sc, near, near_c, y1, y1_c, w2, *rest):
    sum_p, sum_q, w2_lo, w2_hi = rest[-4:]
    half = w2_lo.shape[0]
    w2_lo[...] = w2[:half]
    w2_hi[...] = w2[half:]

    @pl.when(here[0] % 2 == 1)
    def _():
        far_sums(sc, near, near_c, y1, y1_c, w2, *rest[:-4], sum_p, sum_q)


def rest_body(
    sc, here, img, txt, p, w2_lo_c, w2_hi_c, u_p, v_p, sum_p, img_grad, txt_grad, total, held, sems
):
    half = p.shape[0] // 2
    own = (u_p[...], [v_p[3:4, :half], v_p[3:4, half:]])
    total[...] = sum_p[...] + terms(p[...], [w2_lo_c[...], w2_hi_c[...]], sc, own)
    write_out(here[0] >= 2, img, txt, lambda part: total[part], img_grad, txt_grad, held, sems)


def last_body(here, img, txt, sum_q, back, _img, _txt, img_grad, txt_grad, held, sems):
    def dunit(part):
        return sum_q[part] + back[part].astype(jnp.float32)

    write_out(here[0] < 2, img, txt, dunit, img_grad, txt_grad, held, sems)


def local(picture_vectors, caption_vectors, caption_position, sharpness_factor, affine_offset):
    groups = lax.axis_size("loop")
    rows, depth = picture_vectors.shape
    half = rows // 2
    img, txt, scale, shift = picture_vectors, caption_vectors, sharpness_factor, affine_offset

    def swap(to):
        pairs = []
        for g in range(groups):
            for n in range(4):
                h, m = to(g, n)
                pairs.append((g * 4 + n, (h % groups) * 4 + m))
        def go(x, name):
            with jax.named_scope(name):
                return lax.ppermute(x, AXES, pairs)

        return go

    core = swap(lambda g, n: (g, n ^ 1))
    chip = swap(lambda g, n: (g, n ^ 2))
    group = swap(lambda g, n: (g + 1, n - 2) if n >= 2 else (g - 1, n + 2))

    def of(shape, dtype=jnp.float32):
        return jax.ShapeDtypeStruct(shape, dtype)

    here = lax.axis_index("narrow").astype(jnp.int32).reshape(1)
    bf16 = jnp.bfloat16
    one, wide = of((rows, depth), bf16), of((rows, depth))
    part, four = of((half, depth), bf16), of((4 * rows, depth), bf16)
    dma = pltpu.SemaphoreType.DMA
    far = lambda x: pltpu.with_memory_space_constraint(x, pltpu.HBM)

    place = (of((rows, 1), jnp.int32), of((4, rows), jnp.int32)) * 2
    pos = far(caption_position)
    reading = [pltpu.VMEM((1, 4 * rows), jnp.int32), dma]
    p, q, *spot = call(
        unit_body,
        (one, one) + place,
        [SMEM] + [HBM] * 3,
        scratch_shapes=reading + [pltpu.VMEM((2, rows, depth), bf16), dma((2,))],
    )(here, far(img), far(txt), pos)
    x2 = chip(q, "chip_q")
    y0 = group(p, "group_p")
    y1 = group(x2, "group_x2")
    w2 = chip(p, "chip_p")

    sc = call(nums_body, of((2, 128)), [SMEM] * 2)(scale, shift)
    match = call(
        match_body,
        place,
        [SMEM, HBM] + [VMEM] * 4,
        scratch_shapes=reading,
        input_output_aliases={2 + j: j for j in range(4)},
    )(here, pos, *spot)
    near = call(join_body, four, [VMEM] * 4)(p, q, x2, y0)
    near_c = core(near, "core_xy")
    own_p, own_q, part_x = call(own_body, (wide,) * 3, [VMEM] * 6)(sc, near, *match)
    y1 = call(take_body, one, [VMEM] * 2)(y1, own_q)
    y1_c = core(y1, "core_y")
    part_x = call(mid_body, wide, [VMEM] * 5)(sc, near, near_c, y1, part_x)
    blocks = (sc, near, near_c, y1, y1_c, w2, *match, own_p, own_q)
    send, sum_p, sum_q = call(late_body, (one, wide, wide), [SMEM] + [VMEM] * 13)(
        here, part_x, *blocks
    )
    back = chip(send, "chip_send")
    sum_p, sum_q, w2_lo, w2_hi = call(
        visit_body,
        (wide, wide, part, part),
        [SMEM] + [VMEM] * 15,
        input_output_aliases={2: 0, 3: 1},
    )(here, send, sum_p, sum_q, *blocks)
    out = [pltpu.VMEM((rows, depth), jnp.float32), dma((4,))]
    grads = call(
        rest_body,
        (wide, wide),
        [VMEM, SMEM] + [VMEM] * 8,
        (HBM, HBM),
        scratch_shapes=[pltpu.VMEM((rows, depth), jnp.float32)] + out,
    )(sc, here, img, txt, p, core(w2_lo, "core_w_lo"), core(w2_hi, "core_w_hi"), *match[:2], sum_p)
    return call(
        last_body,
        (wide, wide),
        [SMEM] + [VMEM] * 4 + [HBM] * 2,
        (HBM, HBM),
        scratch_shapes=out,
        input_output_aliases={5: 0, 6: 1},
    )(here, img, txt, sum_q, back, *grads)


def solution(mesh):
    return jax.shard_map(
        local,
        mesh=mesh,
        in_specs=(
            P(AXES, None),
            P(AXES, None),
            P("loop", None),
            P(),
            P(),
        ),
        out_specs=(P(AXES, None), P(AXES, None)),
        check_vma=False,
    )
```

```python
import jax
import jax.numpy as jnp
from jax import lax
from jax.experimental import pallas as pl
from jax.experimental.pallas import tpu as pltpu
from jax.sharding import PartitionSpec as P

AXES = ("loop", "narrow")
VMEM = pl.BlockSpec(memory_space=pltpu.VMEM)
SMEM = pl.BlockSpec(memory_space=pltpu.SMEM)
HBM = pl.BlockSpec(memory_space=pltpu.HBM)
NT = (((1,), (1,)), ((), ()))
NN = (((1,), (0,)), ((), ()))
COST = {"unit": 16 * 10**9, "take": 64 * 10**9, "last": 64 * 10**9, "nums": 10**9}


def pieces_of(rows):
    half = rows // 2
    first = half // 32 * 16
    edges = [0, first, half, half + first, rows]
    return [(low, high - low) for low, high in zip(edges, edges[1:])]


def inv_norm(values):
    return lax.rsqrt(jnp.sum(values * values, axis=-1, keepdims=True) + 1e-06)


def dot(a, b, dims):
    return lax.dot_general(a, b, dims, preferred_element_type=jnp.float32)


def call(body, out_shape, in_specs, out_specs=None, vmem=6, **kwargs):
    if out_specs is None:
        out_specs = jax.tree.map(lambda _: VMEM, out_shape)
    name = body.__name__.removesuffix("_body")
    return pl.pallas_call(
        body,
        name=name,
        out_shape=out_shape,
        in_specs=in_specs,
        out_specs=out_specs,
        compiler_params=pltpu.CompilerParams(vmem_limit_bytes=vmem * 1024 * 1024),
        cost_estimate=pl.CostEstimate(flops=COST.get(name, 1), bytes_accessed=1, transcendentals=0),
        **kwargs,
    )


def unit_body(here, img, txt, pos_far, p, q, *rest):
    raw, sems = rest[-2:]
    copies = []
    for i, ref in enumerate((img, txt)):
        copies.append(pltpu.make_async_copy(ref, raw.at[i], sems.at[i]))
        copies[-1].start()

    def unit(i):
        copies[i].wait()
        values = raw[i].astype(jnp.float32)
        return (values * inv_norm(values)).astype(jnp.bfloat16)

    @pl.when(here[0] < 2)
    def _():
        p[...] = unit(0)
        q[...] = unit(1)

    @pl.when(here[0] >= 2)
    def _():
        p[...] = unit(1)
        q[...] = unit(0)

    @pl.when(here[0] % 2 == 0)
    def _():
        spots(here, pos_far, *rest[:-2])


def nums_body(scale, shift, sc):
    sc[0:1] = jnp.full((1, sc.shape[1]), scale[0], jnp.float32)
    sc[1:2] = jnp.full((1, sc.shape[1]), shift[0], jnp.float32)


def match_body(here, pos_far, *rest):
    @pl.when(here[0] % 2 == 1)
    def _():
        spots(here, pos_far, *rest[4:])


def spots(here, pos_far, u_p, v_p, u_q, v_q, pos, sem):
    rows = u_p.shape[0]
    copy = pltpu.make_async_copy(pos_far, pos, sem)
    copy.start()
    copy.wait()
    me = here[0]
    lane = lax.broadcasted_iota(jnp.int32, (1, rows), 1)
    square = (rows, rows)
    diagonal = lax.broadcasted_iota(jnp.int32, square, 0) == lax.broadcasted_iota(
        jnp.int32, square, 1
    )

    def column(row):
        spread = jnp.where(diagonal, jnp.broadcast_to(row, square).astype(jnp.float32), 0.0)
        return jnp.sum(spread, axis=1, keepdims=True).astype(jnp.int32)

    blocks = [pos[:, k * rows : (k + 1) * rows] for k in range(4)]
    matches, places = [], []
    for j in range(4):
        them = me ^ j
        match = blocks[0]
        for k in range(1, 4):
            match = jnp.where(them == k, blocks[k], match)
        matches.append(match)
        places.append(them * rows + lane)

    def put(u_img, v_img, u_txt, v_txt):
        u_img[...] = column(matches[0])
        u_txt[...] = column(places[0])
        for j in range(4):
            v_img[j : j + 1] = places[j]
            v_txt[j : j + 1] = matches[j]

    @pl.when(me < 2)
    def _():
        put(u_p, v_p, u_q, v_q)

    @pl.when(me >= 2)
    def _():
        put(u_q, v_q, u_p, v_p)


def terms(x, ys, sc, positive=None):
    scale, shift = sc[0:1, 0:1], sc[1:2, 0:1]
    logits = [scale * dot(x, y, NT) + shift for y in ys]
    weights = []
    for j, logit in enumerate(logits):
        g = lax.logistic(logit)
        if positive is not None:
            u, v = positive
            g = g - (u == v[j]).astype(jnp.float32)
        weights.append((scale * g).astype(jnp.bfloat16))
    total = None
    for g, y in zip(weights, ys):
        term = dot(g, y, NN)
        total = term if total is None else total + term
    return total


def join_body(p, q, x2, y0, out):
    rows = p.shape[0]
    for j, part in enumerate((p, q, x2, y0)):
        out[j * rows : (j + 1) * rows] = part[...]


def own_body(sc, near, u_p, v_p, u_q, v_q, sum_p, sum_q, part):
    x, y, x2, y0 = (block(near, j) for j in range(4))
    part[...] = terms(x2, [y0], sc)
    sum_p[...] = terms(x, [y], sc, (u_p[...], [v_p[0:1]])) + terms(x, [y0], sc)
    sum_q[...] = terms(y, [x, x2], sc, (u_q[...], [v_q[0:1], v_q[2:3]]))


def take_body(y, _sum, out):
    out[...] = y[...]


def block(ref, j):
    rows = ref.shape[0] // 4
    return ref[j * rows : (j + 1) * rows]


def mid_body(sc, near, near_c, y1, part, out):
    out[...] = part[...] + terms(block(near, 2), [block(near_c, 3), y1[...]], sc)


def far_sums(sc, near, near_c, y1, y1_c, w2, u_p, v_p, u_q, v_q, own_p, own_q, sum_p, sum_q):
    x, y = block(near, 0), block(near, 1)
    x_c, y_c, x2_c, y0_c = (block(near_c, j) for j in range(4))
    none = jnp.full((1, x.shape[0]), -1, jnp.int32)
    columns = [v_p[1:2], v_p[2:3], none, none, none]
    blocks = [y_c, w2[...], y0_c, y1[...], y1_c[...]]
    sum_p[...] = own_p[...] + terms(x, blocks, sc, (u_p[...], columns))
    own = (u_q[...], [v_q[1:2], v_q[3:4]])
    sum_q[...] = own_q[...] + terms(y, [x_c, x2_c], sc, own)


def late_body(here, part, sc, near, near_c, y1, y1_c, *rest):
    out, sum_p, sum_q = rest[-3:]

    @pl.when(here[0] % 2 == 0)
    def _():
        far_sums(sc, near, near_c, y1, y1_c, *rest[:-3], sum_p, sum_q)

    out[...] = (part[...] + terms(block(near, 2), [y1_c[...]], sc)).astype(out.dtype)


def tangent(raw, dunit):
    values = raw.astype(jnp.float32)
    inv = inv_norm(values)
    unit = values * inv
    return (dunit - unit * jnp.sum(unit * dunit, axis=-1, keepdims=True)) * inv


def write_out(is_txt, img, txt, dunit, img_grad, txt_grad, held, sems):
    def go(raw, grad):
        copies = []
        for j, (start, size) in enumerate(pieces_of(raw.shape[0])):
            part = pl.ds(start, size)
            held[part] = tangent(raw[part], dunit(part))
            copies.append(pltpu.make_async_copy(held.at[part], grad.at[part], sems.at[j]))
            copies[-1].start()
        for copy in copies:
            copy.wait()

    @pl.when(jnp.logical_not(is_txt))
    def _():
        go(img, img_grad)

    @pl.when(is_txt)
    def _():
        go(txt, txt_grad)


def visit_body(here, _send, _sum_p, _sum_q, sc, near, near_c, y1, y1_c, w2, *rest):
    sum_p, sum_q, w2_lo, w2_hi = rest[-4:]
    half = w2_lo.shape[0]
    w2_lo[...] = w2[:half]
    w2_hi[...] = w2[half:]

    @pl.when(here[0] % 2 == 1)
    def _():
        far_sums(sc, near, near_c, y1, y1_c, w2, *rest[:-4], sum_p, sum_q)


def rest_body(
    sc, here, img, txt, p, w2_lo_c, w2_hi_c, u_p, v_p, sum_p, img_grad, txt_grad, total, held, sems
):
    half = p.shape[0] // 2
    own = (u_p[...], [v_p[3:4, :half], v_p[3:4, half:]])
    total[...] = sum_p[...] + terms(p[...], [w2_lo_c[...], w2_hi_c[...]], sc, own)
    write_out(here[0] >= 2, img, txt, lambda part: total[part], img_grad, txt_grad, held, sems)


def last_body(here, img, txt, sum_q, back, _img, _txt, img_grad, txt_grad, held, sems):
    def dunit(part):
        return sum_q[part] + back[part].astype(jnp.float32)

    write_out(here[0] < 2, img, txt, dunit, img_grad, txt_grad, held, sems)


def local(picture_vectors, caption_vectors, caption_position, sharpness_factor, affine_offset):
    groups = lax.axis_size("loop")
    rows, depth = picture_vectors.shape
    half = rows // 2
    img, txt, scale, shift = picture_vectors, caption_vectors, sharpness_factor, affine_offset

    def swap(to):
        pairs = []
        for g in range(groups):
            for n in range(4):
                h, m = to(g, n)
                pairs.append((g * 4 + n, (h % groups) * 4 + m))
        def go(x, name):
            with jax.named_scope(name):
                return lax.ppermute(x, AXES, pairs)

        return go

    core = swap(lambda g, n: (g, n ^ 1))
    chip = swap(lambda g, n: (g, n ^ 2))
    group = swap(lambda g, n: (g + 1, n - 2) if n >= 2 else (g - 1, n + 2))

    def of(shape, dtype=jnp.float32):
        return jax.ShapeDtypeStruct(shape, dtype)

    here = lax.axis_index("narrow").astype(jnp.int32).reshape(1)
    bf16 = jnp.bfloat16
    one, wide = of((rows, depth), bf16), of((rows, depth))
    part, four = of((half, depth), bf16), of((4 * rows, depth), bf16)
    dma = pltpu.SemaphoreType.DMA
    far = lambda x: pltpu.with_memory_space_constraint(x, pltpu.HBM)

    place = (of((rows, 1), jnp.int32), of((4, rows), jnp.int32)) * 2
    pos = far(caption_position)
    reading = [pltpu.VMEM((1, 4 * rows), jnp.int32), dma]
    p, q, *spot = call(
        unit_body,
        (one, one) + place,
        [SMEM] + [HBM] * 3,
        scratch_shapes=reading + [pltpu.VMEM((2, rows, depth), bf16), dma((2,))],
    )(here, far(img), far(txt), pos)
    x2 = chip(q, "chip_q")
    y0 = group(p, "group_p")
    y1 = group(x2, "group_x2")
    w2 = chip(p, "chip_p")

    sc = call(nums_body, of((2, 128)), [SMEM] * 2)(scale, shift)
    match = call(
        match_body,
        place,
        [SMEM, HBM] + [VMEM] * 4,
        scratch_shapes=reading,
        input_output_aliases={2 + j: j for j in range(4)},
    )(here, pos, *spot)
    near = call(join_body, four, [VMEM] * 4)(p, q, x2, y0)
    near_c = core(near, "core_xy")
    own_p, own_q, part_x = call(own_body, (wide,) * 3, [VMEM] * 6)(sc, near, *match)
    y1 = call(take_body, one, [VMEM] * 2)(y1, own_q)
    y1_c = core(y1, "core_y")
    part_x = call(mid_body, wide, [VMEM] * 5)(sc, near, near_c, y1, part_x)
    blocks = (sc, near, near_c, y1, y1_c, w2, *match, own_p, own_q)
    send, sum_p, sum_q = call(late_body, (one, wide, wide), [SMEM] + [VMEM] * 13)(
        here, part_x, *blocks
    )
    back = chip(send, "chip_send")
    sum_p, sum_q, w2_lo, w2_hi = call(
        visit_body,
        (wide, wide, part, part),
        [SMEM] + [VMEM] * 15,
        input_output_aliases={2: 0, 3: 1},
    )(here, send, sum_p, sum_q, *blocks)
    out = [pltpu.VMEM((rows, depth), jnp.float32), dma((4,))]
    grads = call(
        rest_body,
        (wide, wide),
        [VMEM, SMEM] + [VMEM] * 8,
        (HBM, HBM),
        scratch_shapes=[pltpu.VMEM((rows, depth), jnp.float32)] + out,
    )(sc, here, img, txt, p, core(w2_lo, "core_w_lo"), core(w2_hi, "core_w_hi"), *match[:2], sum_p)
    return call(
        last_body,
        (wide, wide),
        [SMEM] + [VMEM] * 4 + [HBM] * 2,
        (HBM, HBM),
        scratch_shapes=out,
        input_output_aliases={5: 0, 6: 1},
    )(here, img, txt, sum_q, back, *grads)


def solution(mesh):
    return jax.shard_map(
        local,
        mesh=mesh,
        in_specs=(
            P(AXES, None),
            P(AXES, None),
            P("loop", None),
            P(),
            P(),
        ),
        out_specs=(P(AXES, None), P(AXES, None)),
        check_vma=False,
    )
```
